32 devices in a mesh: grp: 4 (over z), blk: 8 (over y, x, core).
Axes of the slice: x: 2, y: 2, z: 4, core: 2. Of those that a mesh axis runs over, the one named last changes fastest.
Arguments:
- embeddings: bfloat16 [4, 512, 1024], P('grp', 'blk'), may hold values from -72 to 72
- cluster_ids: int32 [4, 512], P('grp', 'blk'), may hold values from 0 to 15, never falling along the last dimension, each value on 1 to 128 neighbouring positions
- block_list: int32 [4, 64, 2], P('grp', 'blk'), may hold values from 0 to 7, as said below
- block_counts: int32 [4, 8], P('grp', 'blk'), may hold values from 1 to 8, as said below
- pair_targets: float32 [4, 64, 4096], P('grp', 'blk'), may hold values from -6 to 6
- w_left: bfloat16 [1024, 512], replicated, may hold values from -0.125 to 0.125
- w_right: bfloat16 [1024, 512], replicated, may hold values from -0.125 to 0.125
- hidden_bias: float32 [512], replicated, may hold values from -3 to 3
- w_middle: bfloat16 [512, 128], replicated, may hold values from -0.25 to 0.25
- w_final: float32 [128], replicated, may hold values from -0.5 to 0.5
Outputs:
- grad_embeddings: float32 [4, 512, 1024], P('grp', 'blk')
- grad_left: float32 [1024, 512], replicated
- grad_right: float32 [1024, 512], replicated
- grad_bias: float32 [512], replicated
- grad_middle: float32 [512, 128], replicated
- grad_final: float32 [128], replicated
The draws below stay inside these ranges and needn't reach their ends.
Inputs may be any that keep to these rules, and one draw needn't show every extreme that they name: `block_list`: entries are panels of the device's own group; the column panel lies within one of the row panel. `block_counts`: slots of a device at and beyond its count are unused; in every group one device has exactly 8.
All inputs are finite; a program needn't handle non-finite values.
Results may differ from the reference program's by a relative error of at most 0.012.
Values may be sent and summed in bfloat16 or wider, within the bound.
A program may use at most 128 MiB of HBM per device.

```python
import math
import jax
import jax.numpy as jnp
import numpy as np
from jax import lax

D = 1024
H1 = 512
H2 = 128
PANEL = 64
B_DEV = 8
M_DEV = 64
PANELS = 8
MOL_G = 512
N_GRP = 4
N_BLK = 8


def draw_embeddings(key, part):
    base = jnp.clip(jax.random.normal(jax.random.fold_in(key, 5), (N_GRP, MOL_G, D), jnp.float32), -6.0, 6.0)
    period = min(D, N_GRP * N_BLK)
    owner = jnp.arange(N_GRP, dtype=jnp.int32)[:, None] * N_BLK + jnp.arange(MOL_G, dtype=jnp.int32)[None, :] // M_DEV
    column = jnp.arange(D, dtype=jnp.int32)
    marked = column[None, None, :] % period == owner[:, :, None] % period
    return jnp.where(marked, 12.0 * base, base).astype(jnp.bfloat16)


def draw_block_list(key, part):
    key_row, key_offset = jax.random.split(jax.random.fold_in(key, 11))
    row_panel = jax.random.randint(key_row, (N_GRP, N_BLK * B_DEV), 0, PANELS)
    offset = jax.random.randint(key_offset, (N_GRP, N_BLK * B_DEV), -1, 2)
    col_panel = jnp.clip(row_panel + offset, 0, PANELS - 1)
    return jnp.stack([row_panel, col_panel], axis=-1).astype(jnp.int32)


def draw_block_counts(key, part):
    key_count, key_full = jax.random.split(jax.random.fold_in(key, 23))
    counts = jax.random.randint(key_count, (N_GRP, N_BLK), 1, B_DEV + 1)
    fullest = jax.random.randint(key_full, (N_GRP, 1), 0, N_BLK)
    positions = jnp.arange(N_BLK, dtype=jnp.int32)[None, :]
    return jnp.where(positions == fullest, B_DEV, counts).astype(jnp.int32)


def block_scale(rng, shape, cuts, least, largest):
    factor_of = 1.0
    for axis_at, blocks in cuts:
        steps = jax.random.uniform(jax.random.fold_in(jax.random.fold_in(rng, 6), axis_at), (blocks,), jnp.float32, least / len(cuts), largest / len(cuts))
        factor_of = factor_of * jnp.repeat(jnp.exp(steps), shape[axis_at] // blocks).reshape((-1,) + (1,) * (len(shape) - 1 - axis_at))
    return factor_of


def split_up(count, total, bound, lean):
    weights = [(1 << 20) // math.isqrt(rank ** lean) + 1 for rank in range(2, count + 1)]
    surplus, holding = total - bound - (count - 1), [1] * (count - 1)
    while surplus > 0:
        movable = [i for i in range(count - 1) if holding[i] < bound]
        pool, left = sum([weights[i] for i in movable]), surplus
        for i in movable:
            more = min(bound - holding[i], max(1, left * weights[i] // pool), surplus)
            holding[i] = holding[i] + more
            surplus = surplus - more
    return np.array([bound] + holding)


def uneven(own_key, count, total, limit, skew):
    if count == 2:
        one = jax.random.randint(own_key, (), max(1, total - limit), min(limit, total - 1) + 1)
        return jnp.stack([one, total - one])
    sizes = jnp.asarray(split_up(count, total, limit, skew), jnp.int32)
    couples = (count - 1) // 2
    donor, receiver = sizes[1:1 + 2 * couples:2], sizes[2:2 + 2 * couples:2]
    margin = jnp.minimum(donor - 1, limit - receiver)
    shifted = jax.random.randint(jax.random.fold_in(own_key, 1), (couples,), 0, 1 << 20) % (margin + 1)
    sizes = sizes.at[1:1 + 2 * couples:2].set(donor - shifted).at[2:2 + 2 * couples:2].set(receiver + shifted)
    return sizes[jax.random.permutation(jax.random.fold_in(own_key, 2), count)]


def scatter_about(stream_key, extent, spread, most, cuts=(), kind=jnp.bfloat16):
    gain = block_scale(stream_key, extent, cuts, -0.22, 0.18) if cuts else 1.0
    entries = jax.random.normal(stream_key, extent, jnp.float32) * spread * gain
    return jnp.minimum(jnp.maximum(entries, -most), most).astype(kind)


def setup_inputs(seed: int = 0) -> dict:
    streams_of = jax.random.split(jax.random.key(seed), 11)
    embeddings = draw_embeddings(jax.random.fold_in(streams_of[10], 71), 0)
    cluster_ids = jax.vmap(lambda own: jnp.searchsorted(jnp.cumsum(uneven(own, 2 * PANELS, MOL_G, 2 * PANEL, 1)), jnp.arange(MOL_G), side="right"))(jax.random.split(streams_of[1], N_GRP)).reshape((N_GRP, MOL_G)).astype(jnp.int32)
    block_list = draw_block_list(jax.random.fold_in(streams_of[10], 71), 0)
    block_counts = draw_block_counts(jax.random.fold_in(streams_of[10], 71), 0)
    pair_targets = scatter_about(streams_of[4], (N_GRP, N_BLK * B_DEV, PANEL * PANEL), 1.0, 6.0, ((0, 4), (1, 8)), jnp.float32)
    w_left = scatter_about(streams_of[5], (D, H1), (2 * D) ** -0.5, 0.125)
    w_right = scatter_about(streams_of[6], (D, H1), (2 * D) ** -0.5, 0.125)
    hidden_bias = scatter_about(streams_of[7], (H1,), 0.5, 3.0, (), jnp.float32)
    w_middle = scatter_about(streams_of[8], (H1, H2), H1 ** -0.5, 0.25)
    w_final = scatter_about(streams_of[9], (H2,), H2 ** -0.5, 0.5, (), jnp.float32)
    return {"embeddings": embeddings, "cluster_ids": cluster_ids, "block_list": block_list, "block_counts": block_counts, "pair_targets": pair_targets, "w_left": w_left, "w_right": w_right, "hidden_bias": hidden_bias, "w_middle": w_middle, "w_final": w_final}


def silu_slope(value):
    sigmoid_value = jax.nn.sigmoid(value)
    return sigmoid_value * (1.0 + value * (1.0 - sigmoid_value))

def pair_block(left_rows, right_rows, left_ids, right_ids, row_start, col_start, pair_target, live_factor, hidden_bias, w_middle, w_final):
    panel_rows = left_rows.shape[0]
    hidden_width = left_rows.shape[1]
    pre_hidden = left_rows.astype(jnp.float32)[:, None, :] + right_rows.astype(jnp.float32)[None, :, :] + hidden_bias
    hidden = jax.nn.silu(pre_hidden).astype(jnp.bfloat16).reshape(panel_rows * panel_rows, hidden_width)
    pre_upper = jnp.dot(hidden, w_middle, preferred_element_type=jnp.float32)
    upper_act = jax.nn.silu(pre_upper)
    predicted = lax.optimization_barrier(jnp.sum(upper_act * w_final, axis=1))
    left_pos = row_start + jnp.arange(panel_rows, dtype=jnp.int32)
    right_pos = col_start + jnp.arange(panel_rows, dtype=jnp.int32)
    same_cluster = (left_ids[:, None] == right_ids[None, :]) & (left_pos[:, None] != right_pos[None, :])
    residual = jnp.where(same_cluster.reshape(-1), predicted - pair_target, 0.0) * live_factor
    pair_slope = 16.0 * residual
    grad_final = lax.optimization_barrier(jnp.sum(upper_act * pair_slope[:, None], axis=0))
    grad_second = (pair_slope[:, None] * w_final[None, :] * silu_slope(pre_upper)).astype(jnp.bfloat16)
    grad_middle = lax.dot_general(hidden, grad_second, (((0,), (0,)), ((), ())), preferred_element_type=jnp.float32)
    grad_hidden = lax.dot_general(grad_second, w_middle, (((1,), (1,)), ((), ())), preferred_element_type=jnp.float32)
    grad_first = grad_hidden.reshape(panel_rows, panel_rows, hidden_width) * silu_slope(pre_hidden)
    return (lax.optimization_barrier(jnp.sum(grad_first, axis=1)), lax.optimization_barrier(jnp.sum(grad_first, axis=0)), lax.optimization_barrier(jnp.sum(grad_first, axis=(0, 1))), grad_middle, grad_final)

def reference(embeddings, cluster_ids, block_list, block_counts, pair_targets, w_left, w_right, hidden_bias, w_middle, w_final):
    acc_left = jnp.zeros((D, H1), jnp.float32)
    acc_right = jnp.zeros((D, H1), jnp.float32)
    acc_bias = jnp.zeros((H1,), jnp.float32)
    acc_middle = jnp.zeros((H1, H2), jnp.float32)
    acc_final = jnp.zeros((H2,), jnp.float32)
    grad_parts = []
    for group in range(N_GRP):
        group_emb = embeddings[group]
        left_all = jnp.dot(group_emb, w_left, preferred_element_type=jnp.float32).astype(jnp.bfloat16)
        right_all = jnp.dot(group_emb, w_right, preferred_element_type=jnp.float32).astype(jnp.bfloat16)
        group_ids = cluster_ids[group]
        group_blocks = block_list[group]
        group_targets = pair_targets[group]
        group_counts = block_counts[group]

        def device_step(carry, device):
            total_left, total_right, sum_bias, sum_middle, sum_final = carry
            live_count = lax.dynamic_index_in_dim(group_counts, device, 0, keepdims=False)

            def slot_step(inner, slot):
                part_left, part_right, in_bias, in_middle, in_final = inner
                slot_row = device * B_DEV + slot
                entry = lax.dynamic_index_in_dim(group_blocks, slot_row, 0, keepdims=False)
                row_start = (entry[0] * PANEL).astype(jnp.int32)
                col_start = (entry[1] * PANEL).astype(jnp.int32)
                pair_target = lax.dynamic_index_in_dim(group_targets, slot_row, 0, keepdims=False)
                live_factor = (slot < live_count).astype(jnp.float32)
                grad_rows, grad_cols, grad_bias, grad_middle, grad_final = pair_block(lax.dynamic_slice_in_dim(left_all, row_start, PANEL, 0), lax.dynamic_slice_in_dim(right_all, col_start, PANEL, 0), lax.dynamic_slice_in_dim(group_ids, row_start, PANEL, 0), lax.dynamic_slice_in_dim(group_ids, col_start, PANEL, 0), row_start, col_start, pair_target, live_factor, hidden_bias, w_middle, w_final)
                current = lax.dynamic_slice_in_dim(part_left, row_start, PANEL, 0)
                part_left = lax.dynamic_update_slice_in_dim(part_left, current + grad_rows, row_start, 0)
                current = lax.dynamic_slice_in_dim(part_right, col_start, PANEL, 0)
                part_right = lax.dynamic_update_slice_in_dim(part_right, current + grad_cols, col_start, 0)
                return ((part_left, part_right, in_bias + grad_bias, in_middle + grad_middle, in_final + grad_final), None)
            empty = jnp.zeros((MOL_G, H1), jnp.float32)
            inner, unused = lax.scan(slot_step, (empty, empty, sum_bias, sum_middle, sum_final), jnp.arange(B_DEV, dtype=jnp.int32))
            part_left, part_right, sum_bias, sum_middle, sum_final = inner
            rounded_left = lax.optimization_barrier(part_left.astype(jnp.bfloat16)).astype(jnp.float32)
            rounded_right = lax.optimization_barrier(part_right.astype(jnp.bfloat16)).astype(jnp.float32)
            return ((total_left + rounded_left, total_right + rounded_right, sum_bias, sum_middle, sum_final), None)
        start_zero = jnp.zeros((MOL_G, H1), jnp.float32)
        carry, unused = lax.scan(device_step, (start_zero, start_zero, acc_bias, acc_middle, acc_final), jnp.arange(N_BLK, dtype=jnp.int32))
        total_left, total_right, acc_bias, acc_middle, acc_final = carry
        left_grad = total_left.astype(jnp.bfloat16)
        right_grad = total_right.astype(jnp.bfloat16)
        grad_group = jnp.dot(left_grad, w_left.T, preferred_element_type=jnp.float32) + jnp.dot(right_grad, w_right.T, preferred_element_type=jnp.float32)
        grad_parts.append(grad_group)
        acc_left = acc_left + jnp.dot(group_emb.T, left_grad, preferred_element_type=jnp.float32)
        acc_right = acc_right + jnp.dot(group_emb.T, right_grad, preferred_element_type=jnp.float32)
    scale = 1.0 / jnp.sqrt(jnp.float32(N_GRP * N_BLK * B_DEV * PANEL))
    return (jnp.stack(grad_parts, axis=0), acc_left * scale, acc_right * scale, acc_bias * scale, acc_middle * scale, acc_final * scale)
```

```python
import functools
import math

import jax
import jax.numpy as jnp
from jax import lax
from jax.experimental import pallas as pl
from jax.experimental.pallas import tpu as pltpu
from jax.sharding import PartitionSpec as P

ROWS = 16
COLS = 32
MESH = pl.DeviceIdType.MESH


def pair_kernel(
    left_ref, right_ref, bias_ref, row_ids_ref, col_ids_ref, target_ref, middle_ref, final_ref,
    left_out, right_out, sums_out,
    left_half, right_half, left_full, right_full, right_acc, row_acc, weight_row, target_row,
    half_middle, left_acc, final_acc,
):
    panel, hidden = left_ref.shape
    span = 3 * panel
    padded = right_acc.shape[0]
    upper = middle_ref.shape[1]
    fold = target_ref.shape[1] - 8
    middle_out = sums_out.at[0:upper, :]
    half_middle[...] = middle_ref[...] * jnp.bfloat16(0.5)
    left = left_ref[...].astype(jnp.float32)
    right = right_ref[...].astype(jnp.float32).reshape(span, hidden) + bias_ref[...]
    left_half[...] = 0.5 * left
    right_half[0:span, :] = 0.5 * right
    right_half[span:padded, :] = jnp.zeros((padded - span, hidden), jnp.float32)
    left_full[...] = left
    right_full[0:span, :] = right + 1.0
    right_full[span:padded, :] = jnp.zeros((padded - span, hidden), jnp.float32)
    right_acc[...] = jnp.zeros_like(right_acc)
    sums_out[...] = jnp.zeros_like(sums_out)
    final_acc[...] = jnp.zeros_like(final_acc)

    row_ids = row_ids_ref[...]
    col_ids = col_ids_ref[...].reshape(span, 128)[:, 0:panel]
    parts, numbers = [], []
    for offset in range(3):
        for lane in range(panel // fold):
            parts.append(target_ref[offset, 0:fold, lane * panel:(lane + 1) * panel])
        numbers.extend([target_ref[offset, fold:fold + 8, 0:panel]] * (panel // 8))
    col_pos = lax.broadcasted_iota(jnp.int32, (span, panel), 0) - panel
    row_pos = lax.broadcasted_iota(jnp.int32, (span, panel), 1)
    used = (col_ids == row_ids) & (col_pos != row_pos)
    counts = jnp.where(used, jnp.concatenate(numbers, axis=0), 0.0) * 16.0
    targets = jnp.where(used, jnp.concatenate(parts, axis=0), 0.0) * 16.0
    tiles = panel // ROWS
    active = jnp.where(counts > 0.0, 1.0, 0.0)
    for tile in range(tiles):
        weight_row[tile, 0:span, :] = counts[:, tile * ROWS:(tile + 1) * ROWS]
        weight_row[tile, span:padded, :] = jnp.zeros((padded - span, ROWS), jnp.float32)
        target_row[tile, 0:span, :] = targets[:, tile * ROWS:(tile + 1) * ROWS]
        target_row[tile, span:padded, :] = jnp.zeros((padded - span, ROWS), jnp.float32)

    where_col = (col_pos + panel).astype(jnp.float32)
    first_map = jnp.where(active > 0.0, where_col, float(padded))
    last_map = jnp.where(active > 0.0, where_col + 1.0, 0.0)
    half_final = 0.5 * final_ref[...]

    for tile in range(tiles):
        lanes = slice(tile * ROWS, (tile + 1) * ROWS)
        first = jnp.min(first_map[:, lanes]).astype(jnp.int32)
        last = jnp.max(last_map[:, lanes]).astype(jnp.int32)
        start = first // 8 * 8
        chunks = jnp.maximum(last - start + COLS - 1, 0) // COLS
        rows = slice(tile * ROWS, (tile + 1) * ROWS)
        row_acc[...] = jnp.zeros_like(row_acc)

        def chunk_step(step, carry):
            cols = pl.ds(pl.multiple_of(start + step * COLS, 8), COLS)
            pairs = ROWS * COLS
            half = left_half[rows, :][:, None, :] + right_half[cols, :][None, :, :]
            plus = left_full[rows, :][:, None, :] + right_full[cols, :][None, :, :]
            gate = 1.0 + jnp.tanh(half)
            act = half * gate
            slope = gate * (plus - act)
            act_low = act.astype(jnp.bfloat16).reshape(pairs, hidden)
            upper_half = jnp.dot(act_low, half_middle[...], preferred_element_type=jnp.float32)
            upper_gate = 1.0 + jnp.tanh(upper_half)
            upper_act = upper_half * upper_gate
            upper_slope = upper_gate * (1.0 + 2.0 * upper_half - upper_act)
            predicted = jnp.sum(upper_act * final_ref[...], axis=1, keepdims=True)
            weights = weight_row[tile, cols, :]
            goal = target_row[tile, cols, :]
            weights = jnp.concatenate([weights[:, a:a + 1] for a in range(ROWS)], axis=0)
            goal = jnp.concatenate([goal[:, a:a + 1] for a in range(ROWS)], axis=0)
            pair_slope = weights * predicted - goal
            final_acc[...] += jnp.sum(
                (upper_act * pair_slope).reshape(pairs // 8, 8, upper), axis=0
            )
            second = (pair_slope * half_final * upper_slope).astype(jnp.bfloat16)
            middle_out[...] += lax.dot_general(
                second, act_low, (((0,), (0,)), ((), ())), preferred_element_type=jnp.float32
            )
            back = lax.dot_general(
                second, half_middle[...], (((1,), (1,)), ((), ())),
                preferred_element_type=jnp.float32,
            )
            grad = back.reshape(ROWS, COLS, hidden) * slope
            row_acc[...] += jnp.sum(grad.reshape(ROWS, COLS // 8, 8, hidden), axis=1)
            right_acc[cols, :] += jnp.sum(grad, axis=0)
            return carry

        lax.fori_loop(0, chunks, chunk_step, 0)
        left_acc[rows, :] = jnp.sum(row_acc[...], axis=1)
    left_out[...] = left_acc[...].astype(jnp.bfloat16)
    sums_out[upper:upper + 1, :] = jnp.sum(left_acc[...], axis=0, keepdims=True)
    sums_out[upper + 1:upper + 2, 0:upper] = jnp.sum(final_acc[...], axis=0, keepdims=True)
    right_out[...] = right_acc[0:span, :].astype(jnp.bfloat16).reshape(3, panel, hidden)


def pair_grads(left, right, bias, row_ids, col_ids, targets, w_middle, w_final):
    panel, hidden = left.shape
    upper = w_middle.shape[1]
    span = 3 * panel
    padded = span + COLS
    f32 = jnp.float32
    return pl.pallas_call(
        pair_kernel,
        out_shape=(
            jax.ShapeDtypeStruct((panel, hidden), jnp.bfloat16),
            jax.ShapeDtypeStruct((3, panel, hidden), jnp.bfloat16),
            jax.ShapeDtypeStruct((upper + 8, hidden), f32),
        ),
        in_specs=[pl.BlockSpec(memory_space=pltpu.VMEM)] * 8,
        out_specs=[pl.BlockSpec(memory_space=pltpu.VMEM)] * 3,
        scratch_shapes=[
            pltpu.VMEM((panel, hidden), f32),
            pltpu.VMEM((padded, hidden), f32),
            pltpu.VMEM((panel, hidden), f32),
            pltpu.VMEM((padded, hidden), f32),
            pltpu.VMEM((padded, hidden), f32),
            pltpu.VMEM((ROWS, 8, hidden), f32),
            pltpu.VMEM((panel // ROWS, padded, ROWS), f32),
            pltpu.VMEM((panel // ROWS, padded, ROWS), f32),
            pltpu.VMEM((hidden, upper), jnp.bfloat16),
            pltpu.VMEM((panel, hidden), f32),
            pltpu.VMEM((8, upper), f32),
        ],
        compiler_params=pltpu.CompilerParams(vmem_limit_bytes=32 * 1024 * 1024),
        name="pair_grads",
    )(left, right, bias[None, :], row_ids, col_ids, targets, w_middle, w_final[None, :])


def reduce_kernel(
    n_grp, n_blk, scale,
    left_ref, right_ref, emb_ref, w_left_ref, w_right_ref,
    emb_out, final_out,
    edge, panels, partial, arrived, mine_g,
    edge_send, edge_recv, g_send, g_recv, gf_send, gf_recv,
    z_send, z_recv, a_send, a_recv, p_send, p_recv, q_send, q_recv,
):
    f32, bf16 = jnp.float32, jnp.bfloat16
    grp, blk = lax.axis_index("grp"), lax.axis_index("blk")
    chips = n_blk // 2
    chip, core = blk // 2, blk % 2
    panel, hidden = left_ref.shape
    width = hidden // n_grp
    twin = chip * 2 + 1 - core

    def copy(src, dst, send, recv, grp_to, blk_to):
        return pltpu.make_async_remote_copy(
            src_ref=src, dst_ref=dst, send_sem=send, recv_sem=recv,
            device_id=(grp_to, blk_to), device_id_type=MESH,
        )

    def plane(step):
        return lax.rem(chip + step, chips) * 2 + core

    def origin(step):
        return lax.rem(chip + chips - step, chips) * 2 + core

    barrier = pltpu.get_barrier_semaphore()

    def greet_blk(step, carry):
        pl.semaphore_signal(
            barrier, inc=1, device_id=(grp, lax.rem(blk + step, n_blk)), device_id_type=MESH
        )
        return carry

    def greet_grp(step, carry):
        pl.semaphore_signal(
            barrier, inc=1, device_id=(lax.rem(grp + step, n_grp), blk), device_id_type=MESH
        )
        return carry

    lax.fori_loop(1, n_blk, greet_blk, 0)
    lax.fori_loop(1, n_grp, greet_grp, 0)
    panels[0, blk] = left_ref[...]
    pl.semaphore_wait(barrier, n_blk - 1 + n_grp - 1)

    to_before = copy(
        right_ref.at[0], edge.at[1], edge_send.at[0], edge_recv.at[1], grp, lax.rem(blk + n_blk - 1, n_blk)
    )
    to_after = copy(
        right_ref.at[2], edge.at[0], edge_send.at[1], edge_recv.at[0], grp, lax.rem(blk + 1, n_blk)
    )
    to_before.start()
    to_after.start()

    def share(half):
        def send(step, carry):
            copy(
                panels.at[half, blk], panels.at[half, blk],
                g_send.at[half, step], g_recv.at[half, step], grp, plane(step),
            ).start()
            return carry
        lax.fori_loop(1, chips, send, 0)
        copy(
            panels.at[half, blk], panels.at[half, blk],
            gf_send.at[half, 0], gf_recv.at[half, 0], grp, twin,
        ).start()

    def forward(half):
        def hand(step, carry):
            slot = panels.at[half, origin(step)]
            copy(slot, slot, g_send.at[half, step], g_recv.at[half, step], grp, plane(step)).wait_recv()
            copy(slot, slot, gf_send.at[half, step], gf_recv.at[half, step], grp, twin).start()
            return carry
        lax.fori_loop(1, chips, hand, 0)

    def multiply(half):
        def take(step, carry):
            slot = panels.at[half, lax.rem(chip + chips - step, chips) * 2 + 1 - core]
            copy(slot, slot, gf_send.at[half, step], gf_recv.at[half, step], grp, twin).wait_recv()
            return carry
        lax.fori_loop(0, chips, take, 0)
        depth = emb_ref.shape[2]
        product = lax.dot_general(
            emb_ref[...].reshape(n_blk * panel, depth), panels[half].reshape(n_blk * panel, hidden),
            (((0,), (0,)), ((), ())), preferred_element_type=f32,
        )
        for part in range(n_grp):
            partial[half, part] = product[:, part * width:(part + 1) * width].astype(bf16)

        def send(step, carry):
            to = lax.rem(grp + step, n_grp)
            copy(
                partial.at[half, to], arrived.at[half, step],
                z_send.at[half, step], z_recv.at[half, step], to, blk,
            ).start()
            return carry
        lax.fori_loop(1, n_grp, send, 0)

    def spread(half, part):
        slot = final_out.at[half, blk, part]

        def send(step, carry):
            copy(
                slot, slot, p_send.at[half, part, step], p_recv.at[half, part, step], grp, plane(step)
            ).start()
            return carry
        lax.fori_loop(1, chips, send, 0)
        copy(slot, slot, q_send.at[half, part, 0], q_recv.at[half, part, 0], grp, twin).start()

    def combine(half):
        total = partial[half, grp].astype(f32)
        for step in range(1, n_grp):
            slot = arrived.at[half, step]
            copy(slot, slot, z_send.at[half, step], z_recv.at[half, step], grp, blk).wait_recv()
            total = total + arrived[half, step].astype(f32)
        final_out[half, blk, grp] = (total * scale).astype(bf16)
        slot = final_out.at[half, blk, grp]

        def send(step, carry):
            copy(
                slot, slot, a_send.at[half, step], a_recv.at[half, step],
                lax.rem(grp + step, n_grp), blk,
            ).start()
            return carry
        lax.fori_loop(1, n_grp, send, 0)
        spread(half, grp)

    share(0)
    to_before.wait_recv()
    to_after.wait_recv()
    right = right_ref[1].astype(f32)
    right = right + jnp.where(blk > 0, edge[0].astype(f32), 0.0)
    right = right + jnp.where(blk < n_blk - 1, edge[1].astype(f32), 0.0)
    panels[1, blk] = right.astype(bf16)
    mine_g[...] = right.astype(bf16)
    share(1)
    forward(0)
    emb_out[...] = lax.dot_general(
        left_ref[...], w_left_ref[...], (((1,), (1,)), ((), ())), preferred_element_type=f32
    )
    multiply(0)
    forward(1)
    emb_out[...] += lax.dot_general(
        mine_g[...], w_right_ref[...], (((1,), (1,)), ((), ())), preferred_element_type=f32
    )
    multiply(1)
    combine(0)
    combine(1)
    for half in range(2):
        def pass_on(step, carry):
            part = lax.rem(grp + n_grp - step, n_grp)
            slot = final_out.at[half, blk, part]
            copy(slot, slot, a_send.at[half, step], a_recv.at[half, step], grp, blk).wait_recv()
            spread(half, part)
            return carry
        lax.fori_loop(1, n_grp, pass_on, 0)

    def hand_on(index, carry):
        half, rest = index // n_grp, lax.rem(index, n_grp)
        part = lax.rem(grp + n_grp - rest, n_grp)

        def hand(step, inner):
            slot = final_out.at[half, origin(step), part]
            copy(
                slot, slot, p_send.at[half, part, step], p_recv.at[half, part, step], grp, plane(step)
            ).wait_recv()
            copy(
                slot, slot, q_send.at[half, part, step], q_recv.at[half, part, step], grp, twin
            ).start()
            return inner
        return lax.fori_loop(1, chips, hand, carry)
    lax.fori_loop(0, 2 * n_grp, hand_on, 0)

    def finish(index, carry):
        half, part = index // n_grp, lax.rem(index, n_grp)

        def end(step, inner):
            slot = final_out.at[half, lax.rem(chip + chips - step, chips) * 2 + 1 - core, part]
            copy(
                slot, slot, q_send.at[half, part, step], q_recv.at[half, part, step], grp, twin
            ).wait()
            return inner
        lax.fori_loop(0, chips, end, 0)

        def sent(step, inner):
            slot = final_out.at[half, blk, part]
            copy(
                slot, slot, p_send.at[half, part, step], p_recv.at[half, part, step], grp, plane(step)
            ).wait_send()
            return inner
        return lax.fori_loop(1, chips, sent, carry)
    lax.fori_loop(0, 2 * n_grp, finish, 0)

    to_before.wait_send()
    to_after.wait_send()
    for half in range(2):
        def g_done(step, carry):
            slot = panels.at[half, blk]
            copy(slot, slot, g_send.at[half, step], g_recv.at[half, step], grp, plane(step)).wait_send()
            return carry
        lax.fori_loop(1, chips, g_done, 0)

        def gf_done(step, carry):
            slot = panels.at[half, blk]
            copy(slot, slot, gf_send.at[half, step], gf_recv.at[half, step], grp, twin).wait_send()
            return carry
        lax.fori_loop(0, chips, gf_done, 0)

        def z_done(step, carry):
            slot = partial.at[half, 0]
            copy(slot, slot, z_send.at[half, step], z_recv.at[half, step], grp, blk).wait_send()
            slot = final_out.at[half, blk, 0]
            copy(slot, slot, a_send.at[half, step], a_recv.at[half, step], grp, blk).wait_send()
            return carry
        lax.fori_loop(1, n_grp, z_done, 0)


def reduce_grads(n_grp, n_blk, scale, left_grad, right_part, emb_cols, w_left, w_right):
    panel, hidden = left_grad.shape
    depth = emb_cols.shape[2]
    wide = w_left.shape[0]
    chips = n_blk // 2
    width = hidden // n_grp
    bf16 = jnp.bfloat16
    dma = pltpu.SemaphoreType.DMA
    return pl.pallas_call(
        functools.partial(reduce_kernel, n_grp, n_blk, scale),
        out_shape=(
            jax.ShapeDtypeStruct((panel, wide), jnp.float32),
            jax.ShapeDtypeStruct((2, n_blk, n_grp, depth, width), bf16),
        ),
        in_specs=[pl.BlockSpec(memory_space=pltpu.VMEM)] * 5,
        out_specs=[pl.BlockSpec(memory_space=pltpu.VMEM)] * 2,
        scratch_shapes=[
            pltpu.VMEM((2, panel, hidden), bf16),
            pltpu.VMEM((2, n_blk, panel, hidden), bf16),
            pltpu.VMEM((2, n_grp, depth, width), bf16),
            pltpu.VMEM((2, n_grp, depth, width), bf16),
            pltpu.VMEM((panel, hidden), bf16),
            dma((2,)), dma((2,)),
            dma((2, chips)), dma((2, chips)), dma((2, chips)), dma((2, chips)),
            dma((2, n_grp)), dma((2, n_grp)), dma((2, n_grp)), dma((2, n_grp)),
            dma((2, n_grp, chips)), dma((2, n_grp, chips)),
            dma((2, n_grp, chips)), dma((2, n_grp, chips)),
        ],
        compiler_params=pltpu.CompilerParams(
            collective_id=1, has_side_effects=True, vmem_limit_bytes=40 * 1024 * 1024
        ),
        name="reduce_grads",
    )(left_grad, right_part, emb_cols, w_left, w_right)


def gather_kernel(
    n_blk,
    emb_ref, w_left_ref, w_right_ref, ids_ref, target_ref, block_ref, count_ref,
    left_out, right_out, ids_out, target_out, emb_out,
    emb_cols, ids_mine, target_mine, target_in,
    e_send, e_recv, t_send, t_recv, r_send, r_recv, i_send, i_recv,
):
    f32, bf16 = jnp.float32, jnp.bfloat16
    grp, blk = lax.axis_index("grp"), lax.axis_index("blk")
    depth = emb_out.shape[2]
    slots, fold, lanes = target_ref.shape
    before, after = lax.rem(blk + n_blk - 1, n_blk), lax.rem(blk + 1, n_blk)

    def copy(src, dst, send, recv, blk_to):
        return pltpu.make_async_remote_copy(
            src_ref=src, dst_ref=dst, send_sem=send, recv_sem=recv,
            device_id=(grp, blk_to), device_id_type=MESH,
        )

    barrier = pltpu.get_barrier_semaphore()

    def greet(step, carry):
        pl.semaphore_signal(
            barrier, inc=1, device_id=(grp, lax.rem(blk + step, n_blk)), device_id_type=MESH
        )
        return carry
    lax.fori_loop(1, n_blk, greet, 0)

    for to in range(n_blk):
        emb_cols[to] = emb_ref[:, to * depth:(to + 1) * depth]
    ids_mine[...] = jnp.broadcast_to(ids_ref[...], ids_mine.shape)
    ids_out[1] = ids_mine[...]

    def sum_pair(index, carry):
        to, offset = index // 3, lax.rem(index, 3)
        total = jnp.zeros((fold, lanes), f32)
        number = jnp.zeros((8, lanes), f32)
        for slot in range(slots):
            row, col = block_ref[slot, 0], block_ref[slot, 1]
            hit = (row == to) & (col - row == offset - 1) & (slot < count_ref[0, 0])
            weight = jnp.where(hit, 1.0, 0.0).astype(f32)
            total = total + weight * target_ref[slot]
            number = number + weight
        target_mine[to, offset, 0:fold, :] = total
        target_mine[to, offset, fold:fold + 8, :] = number
        return carry
    lax.fori_loop(0, 3 * n_blk, sum_pair, 0)
    pl.semaphore_wait(barrier, n_blk - 1)

    right_out[1] = jnp.dot(
        emb_ref[...], w_right_ref[...], preferred_element_type=f32
    ).astype(bf16)
    exchanges = [
        copy(right_out.at[1], right_out.at[2], r_send.at[0], r_recv.at[0], before),
        copy(right_out.at[1], right_out.at[0], r_send.at[1], r_recv.at[1], after),
        copy(ids_mine, ids_out.at[2], i_send.at[0], i_recv.at[0], before),
        copy(ids_mine, ids_out.at[0], i_send.at[1], i_recv.at[1], after),
    ]
    for exchange in exchanges:
        exchange.start()

    def send_targets(step, carry):
        to = lax.rem(blk + step, n_blk)
        copy(target_mine.at[to], target_in.at[step], t_send.at[step], t_recv.at[step], to).start()
        return carry
    lax.fori_loop(1, n_blk, send_targets, 0)

    def send_emb(step, carry):
        to = lax.rem(blk + step, n_blk)
        copy(emb_cols.at[to], emb_out.at[blk], e_send.at[step], e_recv.at[step], to).start()
        return carry
    lax.fori_loop(1, n_blk, send_emb, 0)

    left_out[...] = jnp.dot(emb_ref[...], w_left_ref[...], preferred_element_type=f32).astype(bf16)
    emb_out[blk] = emb_cols[blk]
    target_out[...] = target_mine[blk]

    def take_targets(step, carry):
        slot = target_in.at[step]
        copy(slot, slot, t_send.at[step], t_recv.at[step], blk).wait_recv()
        target_out[...] += target_in[step]
        return carry
    lax.fori_loop(1, n_blk, take_targets, 0)

    def finish(step, carry):
        slot = emb_out.at[lax.rem(blk + n_blk - step, n_blk)]
        copy(slot, slot, e_send.at[step], e_recv.at[step], blk).wait()
        copy(target_mine.at[0], target_in.at[0], t_send.at[step], t_recv.at[step], blk).wait_send()
        return carry
    lax.fori_loop(1, n_blk, finish, 0)
    for exchange in exchanges:
        exchange.wait()


def gather_panels(n_blk, emb, w_left, w_right, ids, targets, blocks, counts):
    f32, bf16 = jnp.float32, jnp.bfloat16
    panel, wide = emb.shape
    hidden = w_left.shape[1]
    fold, lanes = targets.shape[1:]
    depth = wide // n_blk
    dma = pltpu.SemaphoreType.DMA
    vmem, smem = pl.BlockSpec(memory_space=pltpu.VMEM), pl.BlockSpec(memory_space=pltpu.SMEM)
    return pl.pallas_call(
        functools.partial(gather_kernel, n_blk),
        out_shape=(
            jax.ShapeDtypeStruct((panel, hidden), bf16),
            jax.ShapeDtypeStruct((3, panel, hidden), bf16),
            jax.ShapeDtypeStruct((3, panel, 128), f32),
            jax.ShapeDtypeStruct((3, fold + 8, lanes), f32),
            jax.ShapeDtypeStruct((n_blk, panel, depth), bf16),
        ),
        in_specs=[vmem] * 5 + [smem] * 2,
        out_specs=[vmem] * 5,
        scratch_shapes=[
            pltpu.VMEM((n_blk, panel, depth), bf16),
            pltpu.VMEM((panel, 128), f32),
            pltpu.VMEM((n_blk, 3, fold + 8, lanes), f32),
            pltpu.VMEM((n_blk, 3, fold + 8, lanes), f32),
            dma((n_blk,)), dma((n_blk,)), dma((n_blk,)), dma((n_blk,)),
            dma((2,)), dma((2,)), dma((2,)), dma((2,)),
        ],
        compiler_params=pltpu.CompilerParams(
            collective_id=2, has_side_effects=True, vmem_limit_bytes=32 * 1024 * 1024
        ),
        name="gather_panels",
    )(emb, w_left, w_right, ids, targets, blocks, counts)


def local(
    embeddings, cluster_ids, block_list, block_counts, pair_targets,
    w_left, w_right, hidden_bias, w_middle, w_final,
):
    f32, bf16 = jnp.float32, jnp.bfloat16
    n_blk = lax.axis_size("blk")
    n_grp = lax.axis_size("grp")
    emb = embeddings[0]
    panel = emb.shape[0]
    slots = block_list.shape[1]
    hidden = w_left.shape[1]
    upper = w_middle.shape[1]
    fold = panel * panel // 128
    targets = pair_targets[0].reshape(slots, panel, panel // fold, fold)
    targets = targets.transpose(0, 3, 2, 1).reshape(slots, fold, 128)
    ids = cluster_ids[0].astype(f32)
    left, right, col_ids, targets, emb_cols = gather_panels(
        n_blk, emb, w_left, w_right, ids[:, None], targets, block_list[0], block_counts
    )
    left_grad, right_part, sums = pair_grads(
        left, right, hidden_bias, ids[None, :], col_ids, targets, w_middle, w_final
    )
    scale = 1.0 / math.sqrt(n_grp * n_blk * slots * panel)
    grad_local, weight = reduce_grads(
        n_grp, n_blk, scale, left_grad, right_part, emb_cols, w_left, w_right
    )
    sums = lax.psum(sums, ("grp", "blk")) * scale
    weight = weight.astype(f32).transpose(0, 1, 3, 2, 4).reshape(2, emb.shape[1], hidden)
    return (
        grad_local[None],
        weight[0],
        weight[1],
        sums[upper],
        sums[:upper].T,
        sums[upper + 1, :upper],
    )


def solution(mesh):
    return jax.shard_map(
        local,
        mesh=mesh,
        in_specs=(
            P("grp", "blk", None), P("grp", "blk"), P("grp", "blk", None), P("grp", "blk"),
            P("grp", "blk", None), P(), P(), P(), P(), P(),
        ),
        out_specs=(P("grp", "blk", None), P(), P(), P(), P(), P()),
        check_vma=False,
    )
```

```python
import functools
import math

import jax
import jax.numpy as jnp
from jax import lax
from jax.experimental import pallas as pl
from jax.experimental.pallas import tpu as pltpu
from jax.sharding import PartitionSpec as P

ROWS = 16
COLS = 48
MESH = pl.DeviceIdType.MESH


def pair_kernel(
    left_ref, right_ref, bias_ref, row_ids_ref, col_ids_ref, target_ref, middle_ref, final_ref,
    left_out, right_out, sums_out,
    left_half, right_half, left_full, right_full, right_acc, row_acc, weight_row, target_row,
    half_middle, left_acc, final_acc, middle_acc,
):
    panel, hidden = left_ref.shape
    span = 3 * panel
    padded = right_acc.shape[0]
    upper = middle_ref.shape[1]
    fold = target_ref.shape[1] - 8
    half_middle[...] = middle_ref[...] * jnp.bfloat16(0.5)
    left = left_ref[...].astype(jnp.float32)
    right = right_ref[...].astype(jnp.float32).reshape(span, hidden) + bias_ref[...]
    left_half[...] = 0.5 * left
    right_half[0:span, :] = 0.5 * right
    right_half[span:padded, :] = jnp.zeros((padded - span, hidden), jnp.float32)
    left_full[...] = left
    right_full[0:span, :] = right + 1.0
    right_full[span:padded, :] = jnp.zeros((padded - span, hidden), jnp.float32)
    right_acc[...] = jnp.zeros_like(right_acc)
    middle_acc[...] = jnp.zeros_like(middle_acc)
    final_acc[...] = jnp.zeros_like(final_acc)

    row_ids = row_ids_ref[...]
    col_ids = col_ids_ref[...].reshape(span, 128)[:, 0:panel]
    parts, numbers = [], []
    for offset in range(3):
        for lane in range(panel // fold):
            parts.append(target_ref[offset, 0:fold, lane * panel:(lane + 1) * panel])
        numbers.extend([target_ref[offset, fold:fold + 8, 0:panel]] * (panel // 8))
    col_pos = lax.broadcasted_iota(jnp.int32, (span, panel), 0) - panel
    row_pos = lax.broadcasted_iota(jnp.int32, (span, panel), 1)
    used = (col_ids == row_ids) & (col_pos != row_pos)
    counts = jnp.where(used, jnp.concatenate(numbers, axis=0), 0.0) * 16.0
    targets = jnp.where(used, jnp.concatenate(parts, axis=0), 0.0) * 16.0
    tiles = panel // ROWS
    active = jnp.where(counts > 0.0, 1.0, 0.0)
    for tile in range(tiles):
        weight_row[tile, 0:span, :] = counts[:, tile * ROWS:(tile + 1) * ROWS]
        weight_row[tile, span:padded, :] = jnp.zeros((padded - span, ROWS), jnp.float32)
        target_row[tile, 0:span, :] = targets[:, tile * ROWS:(tile + 1) * ROWS]
        target_row[tile, span:padded, :] = jnp.zeros((padded - span, ROWS), jnp.float32)

    where_col = (col_pos + panel).astype(jnp.float32)
    first_map = jnp.where(active > 0.0, where_col, float(padded))
    last_map = jnp.where(active > 0.0, where_col + 1.0, 0.0)
    half_final = 0.5 * final_ref[...]

    for tile in range(tiles):
        lanes = slice(tile * ROWS, (tile + 1) * ROWS)
        first = jnp.min(first_map[:, lanes]).astype(jnp.int32)
        last = jnp.max(last_map[:, lanes]).astype(jnp.int32)
        start = first // 8 * 8
        chunks = jnp.maximum(last - start + COLS - 1, 0) // COLS
        rows = slice(tile * ROWS, (tile + 1) * ROWS)
        row_acc[...] = jnp.zeros_like(row_acc)

        def chunk_step(step, carry):
            cols = pl.ds(pl.multiple_of(start + step * COLS, 8), COLS)
            pairs = ROWS * COLS
            half = left_half[rows, :][:, None, :] + right_half[cols, :][None, :, :]
            plus = left_full[rows, :][:, None, :] + right_full[cols, :][None, :, :]
            gate = 1.0 + jnp.tanh(half)
            act = half * gate
            slope = gate * (plus - act)
            act_low = act.astype(jnp.bfloat16).reshape(pairs, hidden)
            upper_half = jnp.dot(act_low, half_middle[...], preferred_element_type=jnp.float32)
            upper_gate = 1.0 + jnp.tanh(upper_half)
            upper_act = upper_half * upper_gate
            upper_slope = upper_gate * (1.0 + 2.0 * upper_half - upper_act)
            predicted = jnp.sum(upper_act * final_ref[...], axis=1, keepdims=True)
            weights = weight_row[tile, cols, :]
            goal = target_row[tile, cols, :]
            weights = jnp.concatenate([weights[:, a:a + 1] for a in range(ROWS)], axis=0)
            goal = jnp.concatenate([goal[:, a:a + 1] for a in range(ROWS)], axis=0)
            pair_slope = weights * predicted - goal
            final_acc[...] += jnp.sum(
                (upper_act * pair_slope).reshape(pairs // 8, 8, upper), axis=0
            )
            second = (pair_slope * half_final * upper_slope).astype(jnp.bfloat16)
            middle_acc[...] += lax.dot_general(
                second, act_low, (((0,), (0,)), ((), ())), preferred_element_type=jnp.float32
            )
            back = lax.dot_general(
                second, half_middle[...], (((1,), (1,)), ((), ())),
                preferred_element_type=jnp.float32,
            )
            grad = back.reshape(ROWS, COLS, hidden) * slope
            row_acc[...] += jnp.sum(grad.reshape(ROWS, COLS // 8, 8, hidden), axis=1)
            right_acc[cols, :] += jnp.sum(grad, axis=0)
            return carry

        lax.fori_loop(0, chunks, chunk_step, 0)
        left_acc[rows, :] = jnp.sum(row_acc[...], axis=1)
    left_out[...] = left_acc[...].astype(jnp.bfloat16)
    sums_out[0:upper, :] = middle_acc[...].astype(jnp.bfloat16)
    bias_row = jnp.sum(left_acc[...], axis=0, keepdims=True)
    final_row = jnp.sum(final_acc[...], axis=0, keepdims=True)
    final_row = jnp.concatenate([final_row] * (hidden // upper), axis=1)
    row_at = lax.broadcasted_iota(jnp.int32, (16, hidden), 0)
    sums_out[upper:upper + 16, :] = jnp.where(row_at == 0, bias_row, final_row).astype(jnp.bfloat16)
    right_out[...] = right_acc[0:span, :].astype(jnp.bfloat16).reshape(3, panel, hidden)


def pair_grads(left, right, bias, row_ids, col_ids, targets, w_middle, w_final):
    panel, hidden = left.shape
    upper = w_middle.shape[1]
    span = 3 * panel
    padded = span + COLS
    f32 = jnp.float32
    return pl.pallas_call(
        pair_kernel,
        out_shape=(
            jax.ShapeDtypeStruct((panel, hidden), jnp.bfloat16),
            jax.ShapeDtypeStruct((3, panel, hidden), jnp.bfloat16),
            jax.ShapeDtypeStruct((upper + 16, hidden), jnp.bfloat16),
        ),
        in_specs=[pl.BlockSpec(memory_space=pltpu.VMEM)] * 8,
        out_specs=[pl.BlockSpec(memory_space=pltpu.VMEM)] * 3,
        scratch_shapes=[
            pltpu.VMEM((panel, hidden), f32),
            pltpu.VMEM((padded, hidden), f32),
            pltpu.VMEM((panel, hidden), f32),
            pltpu.VMEM((padded, hidden), f32),
            pltpu.VMEM((padded, hidden), f32),
            pltpu.VMEM((ROWS, 8, hidden), f32),
            pltpu.VMEM((panel // ROWS, padded, ROWS), f32),
            pltpu.VMEM((panel // ROWS, padded, ROWS), f32),
            pltpu.VMEM((hidden, upper), jnp.bfloat16),
            pltpu.VMEM((panel, hidden), f32),
            pltpu.VMEM((8, upper), f32),
            pltpu.VMEM((upper, hidden), f32),
        ],
        compiler_params=pltpu.CompilerParams(vmem_limit_bytes=32 * 1024 * 1024),
        name="pair_grads",
    )(left, right, bias[None, :], row_ids, col_ids, targets, w_middle, w_final[None, :])


def reduce_kernel(
    n_grp, n_blk, scale,
    left_ref, right_ref, emb_ref, w_left_ref, w_right_ref, sums_ref,
    emb_out, final_out, small_out,
    edge, panels, partial, arrived, mine_g, small, small_in, small_z,
    edge_send, edge_recv, g_send, g_recv, gf_send, gf_recv,
    z_send, z_recv, a_send, a_recv, p_send, p_recv, q_send, q_recv,
    s_send, s_recv, sz_send, sz_recv, sa_send, sa_recv,
):
    f32, bf16 = jnp.float32, jnp.bfloat16
    grp, blk = lax.axis_index("grp"), lax.axis_index("blk")
    chips = n_blk // 2
    chip, core = blk // 2, blk % 2
    panel, hidden = left_ref.shape
    width = hidden // n_grp
    twin = chip * 2 + 1 - core

    def copy(src, dst, send, recv, grp_to, blk_to):
        return pltpu.make_async_remote_copy(
            src_ref=src, dst_ref=dst, send_sem=send, recv_sem=recv,
            device_id=(grp_to, blk_to), device_id_type=MESH,
        )

    def plane(step):
        return lax.rem(chip + step, chips) * 2 + core

    def origin(step):
        return lax.rem(chip + chips - step, chips) * 2 + core

    barrier = pltpu.get_barrier_semaphore()

    def greet_blk(step, carry):
        pl.semaphore_signal(
            barrier, inc=1, device_id=(grp, lax.rem(blk + step, n_blk)), device_id_type=MESH
        )
        return carry

    def greet_grp(step, carry):
        pl.semaphore_signal(
            barrier, inc=1, device_id=(lax.rem(grp + step, n_grp), blk), device_id_type=MESH
        )
        return carry

    lax.fori_loop(1, n_blk, greet_blk, 0)
    lax.fori_loop(1, n_grp, greet_grp, 0)
    panels[0, blk] = left_ref[...]
    share_of = small.shape[1]
    deep = sums_ref.shape[0] // 16
    for tile in range(n_blk * share_of):
        at = small.at[tile // share_of, tile % share_of]
        if tile < deep * (hidden // 128):
            down, across = tile % deep, tile // deep
            at[...] = sums_ref[down * 16:(down + 1) * 16, across * 128:(across + 1) * 128]
        else:
            at[...] = jnp.zeros((16, 128), bf16)
    pl.semaphore_wait(barrier, n_blk - 1 + n_grp - 1)

    to_before = copy(
        right_ref.at[0], edge.at[1], edge_send.at[0], edge_recv.at[1], grp, lax.rem(blk + n_blk - 1, n_blk)
    )
    to_after = copy(
        right_ref.at[2], edge.at[0], edge_send.at[1], edge_recv.at[0], grp, lax.rem(blk + 1, n_blk)
    )
    to_before.start()
    to_after.start()

    def share(half):
        def send(step, carry):
            copy(
                panels.at[half, blk], panels.at[half, blk],
                g_send.at[half, step], g_recv.at[half, step], grp, plane(step),
            ).start()
            return carry
        lax.fori_loop(1, chips, send, 0)
        copy(
            panels.at[half, blk], panels.at[half, blk],
            gf_send.at[half, 0], gf_recv.at[half, 0], grp, twin,
        ).start()

    def forward(half):
        def hand(step, carry):
            slot = panels.at[half, origin(step)]
            copy(slot, slot, g_send.at[half, step], g_recv.at[half, step], grp, plane(step)).wait_recv()
            copy(slot, slot, gf_send.at[half, step], gf_recv.at[half, step], grp, twin).start()
            return carry
        lax.fori_loop(1, chips, hand, 0)

    def multiply(half):
        def take(step, carry):
            slot = panels.at[half, lax.rem(chip + chips - step, chips) * 2 + 1 - core]
            copy(slot, slot, gf_send.at[half, step], gf_recv.at[half, step], grp, twin).wait_recv()
            return carry
        lax.fori_loop(0, chips, take, 0)
        depth = emb_ref.shape[2]
        product = lax.dot_general(
            emb_ref[...].reshape(n_blk * panel, depth), panels[half].reshape(n_blk * panel, hidden),
            (((0,), (0,)), ((), ())), preferred_element_type=f32,
        )
        for part in range(n_grp):
            partial[half, part] = product[:, part * width:(part + 1) * width].astype(bf16)

        def send(step, carry):
            to = lax.rem(grp + step, n_grp)
            copy(
                partial.at[half, to], arrived.at[half, step],
                z_send.at[half, step], z_recv.at[half, step], to, blk,
            ).start()
            return carry
        lax.fori_loop(1, n_grp, send, 0)

    def spread(half, part):
        slot = final_out.at[half, blk, part]

        def send(step, carry):
            copy(
                slot, slot, p_send.at[half, part, step], p_recv.at[half, part, step], grp, plane(step)
            ).start()
            return carry
        lax.fori_loop(1, chips, send, 0)
        copy(slot, slot, q_send.at[half, part, 0], q_recv.at[half, part, 0], grp, twin).start()

    def combine(half):
        total = partial[half, grp].astype(f32)
        for step in range(1, n_grp):
            slot = arrived.at[half, step]
            copy(slot, slot, z_send.at[half, step], z_recv.at[half, step], grp, blk).wait_recv()
            total = total + arrived[half, step].astype(f32)
        final_out[half, blk, grp] = (total * scale).astype(bf16)
        slot = final_out.at[half, blk, grp]

        def send(step, carry):
            copy(
                slot, slot, a_send.at[half, step], a_recv.at[half, step],
                lax.rem(grp + step, n_grp), blk,
            ).start()
            return carry
        lax.fori_loop(1, n_grp, send, 0)
        spread(half, grp)

    share(0)

    def small_start(step, carry):
        to = lax.rem(blk + step, n_blk)
        copy(small.at[to], small_in.at[step], s_send.at[step], s_recv.at[step], grp, to).start()
        return carry
    lax.fori_loop(1, n_blk, small_start, 0)
    to_before.wait_recv()
    to_after.wait_recv()
    right = right_ref[1].astype(f32)
    right = right + jnp.where(blk > 0, edge[0].astype(f32), 0.0)
    right = right + jnp.where(blk < n_blk - 1, edge[1].astype(f32), 0.0)
    panels[1, blk] = right.astype(bf16)
    mine_g[...] = right.astype(bf16)
    share(1)
    forward(0)
    emb_out[...] = lax.dot_general(
        left_ref[...], w_left_ref[...], (((1,), (1,)), ((), ())), preferred_element_type=f32
    )
    multiply(0)
    small_sum = small[blk].astype(f32)
    for step in range(1, n_blk):
        slot = small_in.at[step]
        copy(slot, slot, s_send.at[step], s_recv.at[step], grp, blk).wait_recv()
        small_sum = small_sum + small_in[step].astype(f32)
    small_z[grp] = small_sum.astype(bf16)

    def small_across(step, carry):
        slot = small_z.at[grp]
        copy(slot, slot, sz_send.at[step], sz_recv.at[step], lax.rem(grp + step, n_grp), blk).start()
        return carry
    lax.fori_loop(1, n_grp, small_across, 0)
    forward(1)
    emb_out[...] += lax.dot_general(
        mine_g[...], w_right_ref[...], (((1,), (1,)), ((), ())), preferred_element_type=f32
    )
    multiply(1)
    combine(0)

    def small_take(step, carry):
        slot = small_z.at[lax.rem(grp + n_grp - step, n_grp)]
        copy(slot, slot, sz_send.at[step], sz_recv.at[step], grp, blk).wait_recv()
        return carry
    lax.fori_loop(1, n_grp, small_take, 0)
    small_total = small_z[0].astype(f32)
    for group in range(1, n_grp):
        small_total = small_total + small_z[group].astype(f32)
    small_out[blk] = small_total.astype(bf16)

    def small_spread(step, carry):
        slot = small_out.at[blk]
        copy(
            slot, slot, sa_send.at[step], sa_recv.at[step], grp, lax.rem(blk + step, n_blk)
        ).start()
        return carry
    lax.fori_loop(1, n_blk, small_spread, 0)
    combine(1)
    for half in range(2):
        def pass_on(step, carry):
            part = lax.rem(grp + n_grp - step, n_grp)
            slot = final_out.at[half, blk, part]
            copy(slot, slot, a_send.at[half, step], a_recv.at[half, step], grp, blk).wait_recv()
            spread(half, part)
            return carry
        lax.fori_loop(1, n_grp, pass_on, 0)

    def hand_on(index, carry):
        half, rest = index // n_grp, lax.rem(index, n_grp)
        part = lax.rem(grp + n_grp - rest, n_grp)

        def hand(step, inner):
            slot = final_out.at[half, origin(step), part]
            copy(
                slot, slot, p_send.at[half, part, step], p_recv.at[half, part, step], grp, plane(step)
            ).wait_recv()
            copy(
                slot, slot, q_send.at[half, part, step], q_recv.at[half, part, step], grp, twin
            ).start()
            return inner
        return lax.fori_loop(1, chips, hand, carry)
    lax.fori_loop(0, 2 * n_grp, hand_on, 0)

    def finish(index, carry):
        half, part = index // n_grp, lax.rem(index, n_grp)

        def end(step, inner):
            slot = final_out.at[half, lax.rem(chip + chips - step, chips) * 2 + 1 - core, part]
            copy(
                slot, slot, q_send.at[half, part, step], q_recv.at[half, part, step], grp, twin
            ).wait()
            return inner
        lax.fori_loop(0, chips, end, 0)

        def sent(step, inner):
            slot = final_out.at[half, blk, part]
            copy(
                slot, slot, p_send.at[half, part, step], p_recv.at[half, part, step], grp, plane(step)
            ).wait_send()
            return inner
        return lax.fori_loop(1, chips, sent, carry)
    lax.fori_loop(0, 2 * n_grp, finish, 0)

    to_before.wait_send()
    to_after.wait_send()

    def small_end(step, carry):
        slot = small_out.at[lax.rem(blk + n_blk - step, n_blk)]
        copy(slot, slot, sa_send.at[step], sa_recv.at[step], grp, blk).wait()
        copy(small.at[0], small_in.at[0], s_send.at[step], s_recv.at[step], grp, blk).wait_send()
        return carry
    lax.fori_loop(1, n_blk, small_end, 0)

    def small_end_z(step, carry):
        slot = small_z.at[0]
        copy(slot, slot, sz_send.at[step], sz_recv.at[step], grp, blk).wait_send()
        return carry
    lax.fori_loop(1, n_grp, small_end_z, 0)
    for half in range(2):
        def g_done(step, carry):
            slot = panels.at[half, blk]
            copy(slot, slot, g_send.at[half, step], g_recv.at[half, step], grp, plane(step)).wait_send()
            return carry
        lax.fori_loop(1, chips, g_done, 0)

        def gf_done(step, carry):
            slot = panels.at[half, blk]
            copy(slot, slot, gf_send.at[half, step], gf_recv.at[half, step], grp, twin).wait_send()
            return carry
        lax.fori_loop(0, chips, gf_done, 0)

        def z_done(step, carry):
            slot = partial.at[half, 0]
            copy(slot, slot, z_send.at[half, step], z_recv.at[half, step], grp, blk).wait_send()
            slot = final_out.at[half, blk, 0]
            copy(slot, slot, a_send.at[half, step], a_recv.at[half, step], grp, blk).wait_send()
            return carry
        lax.fori_loop(1, n_grp, z_done, 0)


def reduce_grads(n_grp, n_blk, scale, left_grad, right_part, emb_cols, w_left, w_right, sums):
    panel, hidden = left_grad.shape
    depth = emb_cols.shape[2]
    wide = w_left.shape[0]
    chips = n_blk // 2
    width = hidden // n_grp
    share_of = -(-(sums.shape[0] // 16 * (hidden // 128)) // n_blk)
    bf16 = jnp.bfloat16
    dma = pltpu.SemaphoreType.DMA
    return pl.pallas_call(
        functools.partial(reduce_kernel, n_grp, n_blk, scale),
        out_shape=(
            jax.ShapeDtypeStruct((panel, wide), jnp.float32),
            jax.ShapeDtypeStruct((2, n_blk, n_grp, depth, width), bf16),
            jax.ShapeDtypeStruct((n_blk, share_of, 16, 128), bf16),
        ),
        in_specs=[pl.BlockSpec(memory_space=pltpu.VMEM)] * 6,
        out_specs=[pl.BlockSpec(memory_space=pltpu.VMEM)] * 3,
        scratch_shapes=[
            pltpu.VMEM((2, panel, hidden), bf16),
            pltpu.VMEM((2, n_blk, panel, hidden), bf16),
            pltpu.VMEM((2, n_grp, depth, width), bf16),
            pltpu.VMEM((2, n_grp, depth, width), bf16),
            pltpu.VMEM((panel, hidden), bf16),
            pltpu.VMEM((n_blk, share_of, 16, 128), bf16),
            pltpu.VMEM((n_blk, share_of, 16, 128), bf16),
            pltpu.VMEM((n_grp, share_of, 16, 128), bf16),
            dma((2,)), dma((2,)),
            dma((2, chips)), dma((2, chips)), dma((2, chips)), dma((2, chips)),
            dma((2, n_grp)), dma((2, n_grp)), dma((2, n_grp)), dma((2, n_grp)),
            dma((2, n_grp, chips)), dma((2, n_grp, chips)),
            dma((2, n_grp, chips)), dma((2, n_grp, chips)),
            dma((n_blk,)), dma((n_blk,)), dma((n_grp,)), dma((n_grp,)), dma((n_blk,)), dma((n_blk,)),
        ],
        compiler_params=pltpu.CompilerParams(
            collective_id=1, has_side_effects=True, vmem_limit_bytes=40 * 1024 * 1024
        ),
        name="reduce_grads",
    )(left_grad, right_part, emb_cols, w_left, w_right, sums)


def unpack_kernel(scale, pieces_ref, small_ref, left_out, right_out, bias_out, middle_out, final_out):
    f32 = jnp.float32
    blocks, n_grp, depth, width = pieces_ref.shape[1:]
    for half, out in enumerate((left_out, right_out)):
        for block in range(blocks):
            for part in range(n_grp):
                out[block * depth:(block + 1) * depth, part * width:(part + 1) * width] = (
                    pieces_ref[half, block, part].astype(f32)
                )

    @pl.when(pl.program_id(0) == 0)
    def _():
        share_of = small_ref.shape[1]
        upper = middle_out.shape[1]
        deep = upper // 16 + 1

        def tile(down, across):
            at = across * deep + down
            return small_ref[at // share_of, at % share_of].astype(f32) * scale

        for across in range(middle_out.shape[0] // 128):
            lanes = slice(across * 128, (across + 1) * 128)
            rows = jnp.concatenate([tile(down, across) for down in range(deep - 1)], axis=0)
            middle_out[lanes, :] = rows.T
            bias_out[:, lanes] = tile(deep - 1, across)[0:1, :]
        final_out[...] = tile(deep - 1, 0)[1:2, 0:upper]


def unpack_grads(scale, pieces, small, hidden, upper):
    _, n_blk, n_grp, depth, width = pieces.shape
    steps = math.gcd(n_blk, 4)
    blocks = n_blk // steps
    f32 = jnp.float32
    rows = blocks * depth
    return pl.pallas_call(
        functools.partial(unpack_kernel, scale),
        grid=(steps,),
        out_shape=(
            jax.ShapeDtypeStruct((n_blk * depth, hidden), f32),
            jax.ShapeDtypeStruct((n_blk * depth, hidden), f32),
            jax.ShapeDtypeStruct((1, hidden), f32),
            jax.ShapeDtypeStruct((hidden, upper), f32),
            jax.ShapeDtypeStruct((1, upper), f32),
        ),
        in_specs=[
            pl.BlockSpec((2, blocks, n_grp, depth, width), lambda i: (0, i, 0, 0, 0)),
            pl.BlockSpec(small.shape, lambda i: (0, 0, 0, 0)),
        ],
        out_specs=[
            pl.BlockSpec((rows, hidden), lambda i: (i, 0)),
            pl.BlockSpec((rows, hidden), lambda i: (i, 0)),
            pl.BlockSpec((1, hidden), lambda i: (0, 0)),
            pl.BlockSpec((hidden, upper), lambda i: (0, 0)),
            pl.BlockSpec((1, upper), lambda i: (0, 0)),
        ],
        compiler_params=pltpu.CompilerParams(vmem_limit_bytes=24 * 1024 * 1024),
        name="unpack_grads",
    )(pieces, small)


def gather_kernel(
    n_blk,
    emb_ref, w_left_ref, w_right_ref, ids_ref, target_ref, block_ref, count_ref,
    left_out, right_out, ids_out, target_out, emb_out,
    emb_cols, ids_mine, target_mine, target_in, w_both, w_sem,
    e_send, e_recv, t_send, t_recv, r_send, r_recv, i_send, i_recv,
):
    f32, bf16 = jnp.float32, jnp.bfloat16
    grp, blk = lax.axis_index("grp"), lax.axis_index("blk")
    depth = emb_out.shape[2]
    slots, fold, lanes = target_ref.shape
    before, after = lax.rem(blk + n_blk - 1, n_blk), lax.rem(blk + 1, n_blk)

    def copy(src, dst, send, recv, blk_to):
        return pltpu.make_async_remote_copy(
            src_ref=src, dst_ref=dst, send_sem=send, recv_sem=recv,
            device_id=(grp, blk_to), device_id_type=MESH,
        )

    fetch_right = pltpu.make_async_copy(w_right_ref, w_both.at[1], w_sem.at[1])
    fetch_left = pltpu.make_async_copy(w_left_ref, w_both.at[0], w_sem.at[0])
    fetch_right.start()
    fetch_left.start()
    barrier = pltpu.get_barrier_semaphore()

    def greet(step, carry):
        pl.semaphore_signal(
            barrier, inc=1, device_id=(grp, lax.rem(blk + step, n_blk)), device_id_type=MESH
        )
        return carry
    lax.fori_loop(1, n_blk, greet, 0)

    for to in range(n_blk):
        emb_cols[to] = emb_ref[:, to * depth:(to + 1) * depth]
    ids_mine[...] = jnp.broadcast_to(ids_ref[...], ids_mine.shape)
    ids_out[1] = ids_mine[...]

    def sum_pair(index, carry):
        to, offset = index // 3, lax.rem(index, 3)
        total = jnp.zeros((fold, lanes), f32)
        number = jnp.zeros((8, lanes), f32)
        for slot in range(slots):
            row, col = block_ref[slot, 0], block_ref[slot, 1]
            hit = (row == to) & (col - row == offset - 1) & (slot < count_ref[0, 0])
            weight = jnp.where(hit, 1.0, 0.0).astype(f32)
            total = total + weight * target_ref[slot]
            number = number + weight
        target_mine[to, offset, 0:fold, :] = total
        target_mine[to, offset, fold:fold + 8, :] = number
        return carry
    lax.fori_loop(0, 3 * n_blk, sum_pair, 0)
    pl.semaphore_wait(barrier, n_blk - 1)

    def send_targets(step, carry):
        to = lax.rem(blk + step, n_blk)
        copy(target_mine.at[to], target_in.at[step], t_send.at[step], t_recv.at[step], to).start()
        return carry
    lax.fori_loop(1, n_blk, send_targets, 0)
    fetch_right.wait()
    right_out[1] = jnp.dot(
        emb_ref[...], w_both[1], preferred_element_type=f32
    ).astype(bf16)
    exchanges = [
        copy(right_out.at[1], right_out.at[2], r_send.at[0], r_recv.at[0], before),
        copy(right_out.at[1], right_out.at[0], r_send.at[1], r_recv.at[1], after),
        copy(ids_mine, ids_out.at[2], i_send.at[0], i_recv.at[0], before),
        copy(ids_mine, ids_out.at[0], i_send.at[1], i_recv.at[1], after),
    ]
    for exchange in exchanges:
        exchange.start()

    def send_emb(step, carry):
        to = lax.rem(blk + step, n_blk)
        copy(emb_cols.at[to], emb_out.at[blk], e_send.at[step], e_recv.at[step], to).start()
        return carry
    lax.fori_loop(1, n_blk, send_emb, 0)

    fetch_left.wait()
    left_out[...] = jnp.dot(emb_ref[...], w_both[0], preferred_element_type=f32).astype(bf16)
    emb_out[blk] = emb_cols[blk]
    target_out[...] = target_mine[blk]

    def take_targets(step, carry):
        slot = target_in.at[step]
        copy(slot, slot, t_send.at[step], t_recv.at[step], blk).wait_recv()
        target_out[...] += target_in[step]
        return carry
    lax.fori_loop(1, n_blk, take_targets, 0)

    def finish(step, carry):
        slot = emb_out.at[lax.rem(blk + n_blk - step, n_blk)]
        copy(slot, slot, e_send.at[step], e_recv.at[step], blk).wait()
        copy(target_mine.at[0], target_in.at[0], t_send.at[step], t_recv.at[step], blk).wait_send()
        return carry
    lax.fori_loop(1, n_blk, finish, 0)
    for exchange in exchanges:
        exchange.wait()


def gather_panels(n_blk, emb, w_left, w_right, ids, targets, blocks, counts):
    f32, bf16 = jnp.float32, jnp.bfloat16
    panel, wide = emb.shape
    hidden = w_left.shape[1]
    fold, lanes = targets.shape[1:]
    depth = wide // n_blk
    dma = pltpu.SemaphoreType.DMA
    hbm = pl.BlockSpec(memory_space=pl.ANY)
    vmem, smem = pl.BlockSpec(memory_space=pltpu.VMEM), pl.BlockSpec(memory_space=pltpu.SMEM)
    return pl.pallas_call(
        functools.partial(gather_kernel, n_blk),
        out_shape=(
            jax.ShapeDtypeStruct((panel, hidden), bf16),
            jax.ShapeDtypeStruct((3, panel, hidden), bf16),
            jax.ShapeDtypeStruct((3, panel, 128), f32),
            jax.ShapeDtypeStruct((3, fold + 8, lanes), f32),
            jax.ShapeDtypeStruct((n_blk, panel, depth), bf16),
        ),
        in_specs=[vmem, hbm, hbm, vmem, vmem, smem, smem],
        out_specs=[vmem] * 5,
        scratch_shapes=[
            pltpu.VMEM((n_blk, panel, depth), bf16),
            pltpu.VMEM((panel, 128), f32),
            pltpu.VMEM((n_blk, 3, fold + 8, lanes), f32),
            pltpu.VMEM((n_blk, 3, fold + 8, lanes), f32),
            pltpu.VMEM((2, wide, hidden), bf16),
            dma((2,)),
            dma((n_blk,)), dma((n_blk,)), dma((n_blk,)), dma((n_blk,)),
            dma((2,)), dma((2,)), dma((2,)), dma((2,)),
        ],
        compiler_params=pltpu.CompilerParams(
            collective_id=2, has_side_effects=True, vmem_limit_bytes=32 * 1024 * 1024
        ),
        name="gather_panels",
    )(emb, w_left, w_right, ids, targets, blocks, counts)


def local(
    embeddings, cluster_ids, block_list, block_counts, pair_targets,
    w_left, w_right, hidden_bias, w_middle, w_final,
):
    f32, bf16 = jnp.float32, jnp.bfloat16
    n_blk = lax.axis_size("blk")
    n_grp = lax.axis_size("grp")
    emb = embeddings[0]
    panel = emb.shape[0]
    slots = block_list.shape[1]
    hidden = w_left.shape[1]
    upper = w_middle.shape[1]
    fold = panel * panel // 128
    targets = pair_targets[0].reshape(slots, panel, panel // fold, fold)
    targets = targets.transpose(0, 3, 2, 1).reshape(slots, fold, 128)
    ids = cluster_ids[0].astype(f32)
    left, right, col_ids, targets, emb_cols = gather_panels(
        n_blk, emb, w_left, w_right, ids[:, None], targets, block_list[0], block_counts
    )
    left_grad, right_part, sums = pair_grads(
        left, right, hidden_bias, ids[None, :], col_ids, targets, w_middle, w_final
    )
    scale = 1.0 / math.sqrt(n_grp * n_blk * slots * panel)
    grad_local, pieces, small = reduce_grads(
        n_grp, n_blk, scale, left_grad, right_part, emb_cols, w_left, w_right, sums
    )
    grad_left, grad_right, grad_bias, grad_middle, grad_final = unpack_grads(
        scale, pieces, small, hidden, upper
    )
    return grad_local[None], grad_left, grad_right, grad_bias[0], grad_middle, grad_final[0]


def solution(mesh):
    return jax.shard_map(
        local,
        mesh=mesh,
        in_specs=(
            P("grp", "blk", None), P("grp", "blk"), P("grp", "blk", None), P("grp", "blk"),
            P("grp", "blk", None), P(), P(), P(), P(), P(),
        ),
        out_specs=(P("grp", "blk", None), P(), P(), P(), P(), P()),
        check_vma=False,
    )
```

```python
import functools
import math

import jax
import jax.numpy as jnp
from jax import lax
from jax.experimental import pallas as pl
from jax.experimental.pallas import tpu as pltpu
from jax.sharding import PartitionSpec as P

ROWS = 16
COLS = 48
BATCH = 4
MESH = pl.DeviceIdType.MESH


def pair_kernel(
    left_ref, right_ref, bias_ref, row_ids_ref, col_ids_ref, target_ref, middle_ref, final_ref,
    left_out, right_out, sums_out,
    left_half, right_half, left_full, right_full, right_acc, row_acc, weight_row, target_row,
    half_middle, left_acc, final_acc, middle_acc, slope_ref, act_ref, second_ref,
):
    panel, hidden = left_ref.shape
    span = 3 * panel
    padded = right_acc.shape[0]
    upper = middle_ref.shape[1]
    fold = target_ref.shape[1] - 8
    half_middle[...] = middle_ref[...] * jnp.bfloat16(0.5)
    left = left_ref[...].astype(jnp.float32)
    right = right_ref[...].astype(jnp.float32).reshape(span, hidden) + bias_ref[...]
    left_half[...] = 0.5 * left
    right_half[0:span, :] = 0.5 * right
    right_half[span:padded, :] = jnp.zeros((padded - span, hidden), jnp.float32)
    left_full[...] = left
    right_full[0:span, :] = right + 1.0
    right_full[span:padded, :] = jnp.zeros((padded - span, hidden), jnp.float32)
    right_acc[...] = jnp.zeros_like(right_acc)
    middle_acc[...] = jnp.zeros_like(middle_acc)
    final_acc[...] = jnp.zeros_like(final_acc)

    row_ids = row_ids_ref[...]
    col_ids = col_ids_ref[...].reshape(span, 128)[:, 0:panel]
    parts, numbers = [], []
    for offset in range(3):
        for lane in range(panel // fold):
            parts.append(target_ref[offset, 0:fold, lane * panel:(lane + 1) * panel])
        numbers.extend([target_ref[offset, fold:fold + 8, 0:panel]] * (panel // 8))
    col_pos = lax.broadcasted_iota(jnp.int32, (span, panel), 0) - panel
    row_pos = lax.broadcasted_iota(jnp.int32, (span, panel), 1)
    used = (col_ids == row_ids) & (col_pos != row_pos)
    counts = jnp.where(used, jnp.concatenate(numbers, axis=0), 0.0) * 16.0
    targets = jnp.where(used, jnp.concatenate(parts, axis=0), 0.0) * 16.0
    tiles = panel // ROWS
    active = jnp.where(counts > 0.0, 1.0, 0.0)
    for tile in range(tiles):
        weight_row[tile, 0:span, :] = counts[:, tile * ROWS:(tile + 1) * ROWS]
        weight_row[tile, span:padded, :] = jnp.zeros((padded - span, ROWS), jnp.float32)
        target_row[tile, 0:span, :] = targets[:, tile * ROWS:(tile + 1) * ROWS]
        target_row[tile, span:padded, :] = jnp.zeros((padded - span, ROWS), jnp.float32)

    where_col = (col_pos + panel).astype(jnp.float32)
    first_map = jnp.where(active > 0.0, where_col, float(padded))
    last_map = jnp.where(active > 0.0, where_col + 1.0, 0.0)
    half_final = 0.5 * final_ref[...]

    for tile in range(tiles):
        lanes = slice(tile * ROWS, (tile + 1) * ROWS)
        first = jnp.min(first_map[:, lanes]).astype(jnp.int32)
        last = jnp.max(last_map[:, lanes]).astype(jnp.int32)
        start = first // 8 * 8
        chunks = jnp.maximum(last - start + COLS - 1, 0) // COLS
        rows = slice(tile * ROWS, (tile + 1) * ROWS)
        row_acc[...] = jnp.zeros_like(row_acc)

        def chunk_step(step, carry):
            first_col = pl.multiple_of(start + step * COLS, 8)
            cols = pl.ds(first_col, COLS)
            weights = weight_row[tile, cols, :]
            goals = target_row[tile, cols, :]

            def open_part(part):
                for row in range(part * BATCH, (part + 1) * BATCH):
                    at = tile * ROWS + row
                    pairs = slice(row * COLS, (row + 1) * COLS)
                    half = left_half[at:at + 1, :] + right_half[cols, :]
                    plus = left_full[at:at + 1, :] + right_full[cols, :]
                    gate = 1.0 + jnp.tanh(half)
                    act = half * gate
                    slope_ref[pairs, :] = gate * (plus - act)
                    act_ref[pairs, :] = act.astype(jnp.bfloat16)

            def part_pairs(part):
                return slice(part * BATCH * COLS, (part + 1) * BATCH * COLS)

            open_part(0)
            for part in range(ROWS // BATCH):
                pairs = part_pairs(part)
                upper_half = jnp.dot(
                    act_ref[pairs, :], half_middle[...], preferred_element_type=jnp.float32
                )
                if part + 1 < ROWS // BATCH:
                    open_part(part + 1)
                upper_gate = 1.0 + jnp.tanh(upper_half)
                upper_act = upper_half * upper_gate
                upper_slope = upper_gate * (1.0 + 2.0 * upper_half - upper_act)
                predicted = jnp.sum(upper_act * final_ref[...], axis=1, keepdims=True)
                lanes_of = range(part * BATCH, (part + 1) * BATCH)
                weight = jnp.concatenate([weights[:, a:a + 1] for a in lanes_of], axis=0)
                goal = jnp.concatenate([goals[:, a:a + 1] for a in lanes_of], axis=0)
                pair_slope = weight * predicted - goal
                final_acc[...] += jnp.sum(
                    (upper_act * pair_slope).reshape(BATCH * COLS // 8, 8, upper), axis=0
                )
                second = (pair_slope * half_final * upper_slope).astype(jnp.bfloat16)
                second_ref[pairs, :] = second
                back = lax.dot_general(
                    second, half_middle[...], (((1,), (1,)), ((), ())),
                    preferred_element_type=jnp.float32,
                )
                across = jnp.zeros((COLS, hidden), jnp.float32)
                for row in range(BATCH):
                    index = part * BATCH + row
                    grad = back[row * COLS:(row + 1) * COLS, :]
                    grad = grad * slope_ref[index * COLS:(index + 1) * COLS, :]
                    across = across + grad
                    row_acc[index] += jnp.sum(grad.reshape(COLS // 8, 8, hidden), axis=0)
                right_acc[cols, :] += across
            middle_acc[...] += lax.dot_general(
                second_ref[...], act_ref[...], (((0,), (0,)), ((), ())),
                preferred_element_type=jnp.float32,
            )
            return carry

        lax.fori_loop(0, chunks, chunk_step, 0)
        left_acc[rows, :] = jnp.sum(row_acc[...], axis=1)
    left_out[...] = left_acc[...].astype(jnp.bfloat16)
    sums_out[0:upper, :] = middle_acc[...].astype(jnp.bfloat16)
    bias_row = jnp.sum(left_acc[...], axis=0, keepdims=True)
    final_row = jnp.sum(final_acc[...], axis=0, keepdims=True)
    final_row = jnp.concatenate([final_row] * (hidden // upper), axis=1)
    row_at = lax.broadcasted_iota(jnp.int32, (16, hidden), 0)
    sums_out[upper:upper + 16, :] = jnp.where(row_at == 0, bias_row, final_row).astype(jnp.bfloat16)
    right_out[...] = right_acc[0:span, :].astype(jnp.bfloat16).reshape(3, panel, hidden)


def pair_grads(left, right, bias, row_ids, col_ids, targets, w_middle, w_final):
    panel, hidden = left.shape
    upper = w_middle.shape[1]
    span = 3 * panel
    padded = span + COLS
    f32 = jnp.float32
    return pl.pallas_call(
        pair_kernel,
        out_shape=(
            jax.ShapeDtypeStruct((panel, hidden), jnp.bfloat16),
            jax.ShapeDtypeStruct((3, panel, hidden), jnp.bfloat16),
            jax.ShapeDtypeStruct((upper + 16, hidden), jnp.bfloat16),
        ),
        in_specs=[pl.BlockSpec(memory_space=pltpu.VMEM)] * 8,
        out_specs=[pl.BlockSpec(memory_space=pltpu.VMEM)] * 3,
        scratch_shapes=[
            pltpu.VMEM((panel, hidden), f32),
            pltpu.VMEM((padded, hidden), f32),
            pltpu.VMEM((panel, hidden), f32),
            pltpu.VMEM((padded, hidden), f32),
            pltpu.VMEM((padded, hidden), f32),
            pltpu.VMEM((ROWS, 8, hidden), f32),
            pltpu.VMEM((panel // ROWS, padded, ROWS), f32),
            pltpu.VMEM((panel // ROWS, padded, ROWS), f32),
            pltpu.VMEM((hidden, upper), jnp.bfloat16),
            pltpu.VMEM((panel, hidden), f32),
            pltpu.VMEM((8, upper), f32),
            pltpu.VMEM((upper, hidden), f32),
            pltpu.VMEM((ROWS * COLS, hidden), f32),
            pltpu.VMEM((ROWS * COLS, hidden), jnp.bfloat16),
            pltpu.VMEM((ROWS * COLS, upper), jnp.bfloat16),
        ],
        compiler_params=pltpu.CompilerParams(vmem_limit_bytes=32 * 1024 * 1024),
        name="pair_grads",
    )(left, right, bias[None, :], row_ids, col_ids, targets, w_middle, w_final[None, :])


def reduce_kernel(
    n_grp, n_blk, scale,
    left_ref, right_ref, emb_ref, w_left_ref, w_right_ref, sums_ref,
    emb_out, final_out, small_out,
    edge, panels, partial, arrived, mine_g, small, small_in, small_z,
    edge_send, edge_recv, g_send, g_recv, gf_send, gf_recv,
    z_send, z_recv, a_send, a_recv, p_send, p_recv, q_send, q_recv,
    s_send, s_recv, sz_send, sz_recv, sa_send, sa_recv,
):
    f32, bf16 = jnp.float32, jnp.bfloat16
    grp, blk = lax.axis_index("grp"), lax.axis_index("blk")
    chips = n_blk // 2
    chip, core = blk // 2, blk % 2
    panel, hidden = left_ref.shape
    width = hidden // n_grp
    twin = chip * 2 + 1 - core

    def copy(src, dst, send, recv, grp_to, blk_to):
        return pltpu.make_async_remote_copy(
            src_ref=src, dst_ref=dst, send_sem=send, recv_sem=recv,
            device_id=(grp_to, blk_to), device_id_type=MESH,
        )

    def plane(step):
        return lax.rem(chip + step, chips) * 2 + core

    def origin(step):
        return lax.rem(chip + chips - step, chips) * 2 + core

    barrier = pltpu.get_barrier_semaphore()

    def greet_blk(step, carry):
        pl.semaphore_signal(
            barrier, inc=1, device_id=(grp, lax.rem(blk + step, n_blk)), device_id_type=MESH
        )
        return carry

    def greet_grp(step, carry):
        pl.semaphore_signal(
            barrier, inc=1, device_id=(lax.rem(grp + step, n_grp), blk), device_id_type=MESH
        )
        return carry

    lax.fori_loop(1, n_blk, greet_blk, 0)
    lax.fori_loop(1, n_grp, greet_grp, 0)
    panels[0, blk] = left_ref[...]
    share_of = small.shape[1]
    deep = sums_ref.shape[0] // 16
    for tile in range(n_blk * share_of):
        at = small.at[tile // share_of, tile % share_of]
        if tile < deep * (hidden // 128):
            down, across = tile % deep, tile // deep
            at[...] = sums_ref[down * 16:(down + 1) * 16, across * 128:(across + 1) * 128]
        else:
            at[...] = jnp.zeros((16, 128), bf16)
    pl.semaphore_wait(barrier, n_blk - 1 + n_grp - 1)

    to_before = copy(
        right_ref.at[0], edge.at[1], edge_send.at[0], edge_recv.at[1], grp, lax.rem(blk + n_blk - 1, n_blk)
    )
    to_after = copy(
        right_ref.at[2], edge.at[0], edge_send.at[1], edge_recv.at[0], grp, lax.rem(blk + 1, n_blk)
    )
    to_before.start()
    to_after.start()

    def share(half):
        def send(step, carry):
            copy(
                panels.at[half, blk], panels.at[half, blk],
                g_send.at[half, step], g_recv.at[half, step], grp, plane(step),
            ).start()
            return carry
        lax.fori_loop(1, chips, send, 0)
        copy(
            panels.at[half, blk], panels.at[half, blk],
            gf_send.at[half, 0], gf_recv.at[half, 0], grp, twin,
        ).start()

    def forward(half):
        def hand(step, carry):
            slot = panels.at[half, origin(step)]
            copy(slot, slot, g_send.at[half, step], g_recv.at[half, step], grp, plane(step)).wait_recv()
            copy(slot, slot, gf_send.at[half, step], gf_recv.at[half, step], grp, twin).start()
            return carry
        lax.fori_loop(1, chips, hand, 0)

    def multiply(half):
        def take(step, carry):
            slot = panels.at[half, lax.rem(chip + chips - step, chips) * 2 + 1 - core]
            copy(slot, slot, gf_send.at[half, step], gf_recv.at[half, step], grp, twin).wait_recv()
            return carry
        lax.fori_loop(0, chips, take, 0)
        depth = emb_ref.shape[2]
        product = lax.dot_general(
            emb_ref[...].reshape(n_blk * panel, depth), panels[half].reshape(n_blk * panel, hidden),
            (((0,), (0,)), ((), ())), preferred_element_type=f32,
        )
        for part in range(n_grp):
            partial[half, part] = product[:, part * width:(part + 1) * width].astype(bf16)

        def send(step, carry):
            to = lax.rem(grp + step, n_grp)
            copy(
                partial.at[half, to], arrived.at[half, step],
                z_send.at[half, step], z_recv.at[half, step], to, blk,
            ).start()
            return carry
        lax.fori_loop(1, n_grp, send, 0)

    def spread(half, part):
        slot = final_out.at[half, blk, part]

        def send(step, carry):
            copy(
                slot, slot, p_send.at[half, part, step], p_recv.at[half, part, step], grp, plane(step)
            ).start()
            return carry
        lax.fori_loop(1, chips, send, 0)
        copy(slot, slot, q_send.at[half, part, 0], q_recv.at[half, part, 0], grp, twin).start()

    def combine(half):
        total = partial[half, grp].astype(f32)
        for step in range(1, n_grp):
            slot = arrived.at[half, step]
            copy(slot, slot, z_send.at[half, step], z_recv.at[half, step], grp, blk).wait_recv()
            total = total + arrived[half, step].astype(f32)
        final_out[half, blk, grp] = (total * scale).astype(bf16)
        slot = final_out.at[half, blk, grp]

        def send(step, carry):
            copy(
                slot, slot, a_send.at[half, step], a_recv.at[half, step],
                lax.rem(grp + step, n_grp), blk,
            ).start()
            return carry
        lax.fori_loop(1, n_grp, send, 0)
        spread(half, grp)

    share(0)

    def small_start(step, carry):
        to = lax.rem(blk + step, n_blk)
        copy(small.at[to], small_in.at[step], s_send.at[step], s_recv.at[step], grp, to).start()
        return carry
    lax.fori_loop(1, n_blk, small_start, 0)
    to_before.wait_recv()
    to_after.wait_recv()
    right = right_ref[1].astype(f32)
    right = right + jnp.where(blk > 0, edge[0].astype(f32), 0.0)
    right = right + jnp.where(blk < n_blk - 1, edge[1].astype(f32), 0.0)
    panels[1, blk] = right.astype(bf16)
    mine_g[...] = right.astype(bf16)
    share(1)
    forward(0)
    multiply(0)
    forward(1)
    multiply(1)
    combine(0)
    small_sum = small[blk].astype(f32)
    for step in range(1, n_blk):
        slot = small_in.at[step]
        copy(slot, slot, s_send.at[step], s_recv.at[step], grp, blk).wait_recv()
        small_sum = small_sum + small_in[step].astype(f32)
    small_z[grp] = small_sum.astype(bf16)

    def small_across(step, carry):
        slot = small_z.at[grp]
        copy(slot, slot, sz_send.at[step], sz_recv.at[step], lax.rem(grp + step, n_grp), blk).start()
        return carry
    lax.fori_loop(1, n_grp, small_across, 0)

    combine(1)
    for half in range(2):
        def pass_on(step, carry):
            part = lax.rem(grp + n_grp - step, n_grp)
            slot = final_out.at[half, blk, part]
            copy(slot, slot, a_send.at[half, step], a_recv.at[half, step], grp, blk).wait_recv()
            spread(half, part)
            return carry
        lax.fori_loop(1, n_grp, pass_on, 0)

    def small_take(step, carry):
        slot = small_z.at[lax.rem(grp + n_grp - step, n_grp)]
        copy(slot, slot, sz_send.at[step], sz_recv.at[step], grp, blk).wait_recv()
        return carry
    lax.fori_loop(1, n_grp, small_take, 0)
    small_total = small_z[0].astype(f32)
    for group in range(1, n_grp):
        small_total = small_total + small_z[group].astype(f32)
    small_out[blk] = small_total.astype(bf16)

    def small_spread(step, carry):
        slot = small_out.at[blk]
        copy(
            slot, slot, sa_send.at[step], sa_recv.at[step], grp, lax.rem(blk + step, n_blk)
        ).start()
        return carry
    lax.fori_loop(1, n_blk, small_spread, 0)
    def hand_on(index, carry):
        half, rest = index // n_grp, lax.rem(index, n_grp)
        part = lax.rem(grp + n_grp - rest, n_grp)

        def hand(step, inner):
            slot = final_out.at[half, origin(step), part]
            copy(
                slot, slot, p_send.at[half, part, step], p_recv.at[half, part, step], grp, plane(step)
            ).wait_recv()
            copy(
                slot, slot, q_send.at[half, part, step], q_recv.at[half, part, step], grp, twin
            ).start()
            return inner
        return lax.fori_loop(1, chips, hand, carry)
    emb_out[...] = lax.dot_general(
        left_ref[...], w_left_ref[...], (((1,), (1,)), ((), ())), preferred_element_type=f32
    )
    emb_out[...] += lax.dot_general(
        mine_g[...], w_right_ref[...], (((1,), (1,)), ((), ())), preferred_element_type=f32
    )
    lax.fori_loop(0, 2 * n_grp, hand_on, 0)

    def finish(index, carry):
        half, part = index // n_grp, lax.rem(index, n_grp)

        def end(step, inner):
            slot = final_out.at[half, lax.rem(chip + chips - step, chips) * 2 + 1 - core, part]
            copy(
                slot, slot, q_send.at[half, part, step], q_recv.at[half, part, step], grp, twin
            ).wait()
            return inner
        lax.fori_loop(0, chips, end, 0)

        def sent(step, inner):
            slot = final_out.at[half, blk, part]
            copy(
                slot, slot, p_send.at[half, part, step], p_recv.at[half, part, step], grp, plane(step)
            ).wait_send()
            return inner
        return lax.fori_loop(1, chips, sent, carry)
    lax.fori_loop(0, 2 * n_grp, finish, 0)

    to_before.wait_send()
    to_after.wait_send()

    def small_end(step, carry):
        slot = small_out.at[lax.rem(blk + n_blk - step, n_blk)]
        copy(slot, slot, sa_send.at[step], sa_recv.at[step], grp, blk).wait()
        copy(small.at[0], small_in.at[0], s_send.at[step], s_recv.at[step], grp, blk).wait_send()
        return carry
    lax.fori_loop(1, n_blk, small_end, 0)

    def small_end_z(step, carry):
        slot = small_z.at[0]
        copy(slot, slot, sz_send.at[step], sz_recv.at[step], grp, blk).wait_send()
        return carry
    lax.fori_loop(1, n_grp, small_end_z, 0)
    for half in range(2):
        def g_done(step, carry):
            slot = panels.at[half, blk]
            copy(slot, slot, g_send.at[half, step], g_recv.at[half, step], grp, plane(step)).wait_send()
            return carry
        lax.fori_loop(1, chips, g_done, 0)

        def gf_done(step, carry):
            slot = panels.at[half, blk]
            copy(slot, slot, gf_send.at[half, step], gf_recv.at[half, step], grp, twin).wait_send()
            return carry
        lax.fori_loop(0, chips, gf_done, 0)

        def z_done(step, carry):
            slot = partial.at[half, 0]
            copy(slot, slot, z_send.at[half, step], z_recv.at[half, step], grp, blk).wait_send()
            slot = final_out.at[half, blk, 0]
            copy(slot, slot, a_send.at[half, step], a_recv.at[half, step], grp, blk).wait_send()
            return carry
        lax.fori_loop(1, n_grp, z_done, 0)


def reduce_grads(n_grp, n_blk, scale, left_grad, right_part, emb_cols, w_left, w_right, sums):
    panel, hidden = left_grad.shape
    depth = emb_cols.shape[2]
    wide = w_left.shape[0]
    chips = n_blk // 2
    width = hidden // n_grp
    share_of = -(-(sums.shape[0] // 16 * (hidden // 128)) // n_blk)
    bf16 = jnp.bfloat16
    dma = pltpu.SemaphoreType.DMA
    return pl.pallas_call(
        functools.partial(reduce_kernel, n_grp, n_blk, scale),
        out_shape=(
            jax.ShapeDtypeStruct((panel, wide), jnp.float32),
            jax.ShapeDtypeStruct((2, n_blk, n_grp, depth, width), bf16),
            jax.ShapeDtypeStruct((n_blk, share_of, 16, 128), bf16),
        ),
        in_specs=[pl.BlockSpec(memory_space=pltpu.VMEM)] * 6,
        out_specs=[pl.BlockSpec(memory_space=pltpu.VMEM)] * 3,
        scratch_shapes=[
            pltpu.VMEM((2, panel, hidden), bf16),
            pltpu.VMEM((2, n_blk, panel, hidden), bf16),
            pltpu.VMEM((2, n_grp, depth, width), bf16),
            pltpu.VMEM((2, n_grp, depth, width), bf16),
            pltpu.VMEM((panel, hidden), bf16),
            pltpu.VMEM((n_blk, share_of, 16, 128), bf16),
            pltpu.VMEM((n_blk, share_of, 16, 128), bf16),
            pltpu.VMEM((n_grp, share_of, 16, 128), bf16),
            dma((2,)), dma((2,)),
            dma((2, chips)), dma((2, chips)), dma((2, chips)), dma((2, chips)),
            dma((2, n_grp)), dma((2, n_grp)), dma((2, n_grp)), dma((2, n_grp)),
            dma((2, n_grp, chips)), dma((2, n_grp, chips)),
            dma((2, n_grp, chips)), dma((2, n_grp, chips)),
            dma((n_blk,)), dma((n_blk,)), dma((n_grp,)), dma((n_grp,)), dma((n_blk,)), dma((n_blk,)),
        ],
        compiler_params=pltpu.CompilerParams(
            collective_id=1, has_side_effects=True, vmem_limit_bytes=40 * 1024 * 1024
        ),
        name="reduce_grads",
    )(left_grad, right_part, emb_cols, w_left, w_right, sums)


def unpack_kernel(scale, pieces_ref, small_ref, left_out, right_out, bias_out, middle_out, final_out):
    f32 = jnp.float32
    blocks, n_grp, depth, width = pieces_ref.shape[1:]
    for half, out in enumerate((left_out, right_out)):
        for block in range(blocks):
            for part in range(n_grp):
                out[block * depth:(block + 1) * depth, part * width:(part + 1) * width] = (
                    pieces_ref[half, block, part].astype(f32)
                )

    @pl.when(pl.program_id(0) == 0)
    def _():
        share_of = small_ref.shape[1]
        upper = middle_out.shape[1]
        deep = upper // 16 + 1

        def tile(down, across):
            at = across * deep + down
            return small_ref[at // share_of, at % share_of].astype(f32) * scale

        for across in range(middle_out.shape[0] // 128):
            lanes = slice(across * 128, (across + 1) * 128)
            rows = jnp.concatenate([tile(down, across) for down in range(deep - 1)], axis=0)
            middle_out[lanes, :] = rows.T
            bias_out[:, lanes] = tile(deep - 1, across)[0:1, :]
        final_out[...] = tile(deep - 1, 0)[1:2, 0:upper]


def unpack_grads(scale, pieces, small, hidden, upper):
    _, n_blk, n_grp, depth, width = pieces.shape
    steps = math.gcd(n_blk, 4)
    blocks = n_blk // steps
    f32 = jnp.float32
    rows = blocks * depth
    return pl.pallas_call(
        functools.partial(unpack_kernel, scale),
        grid=(steps,),
        out_shape=(
            jax.ShapeDtypeStruct((n_blk * depth, hidden), f32),
            jax.ShapeDtypeStruct((n_blk * depth, hidden), f32),
            jax.ShapeDtypeStruct((1, hidden), f32),
            jax.ShapeDtypeStruct((hidden, upper), f32),
            jax.ShapeDtypeStruct((1, upper), f32),
        ),
        in_specs=[
            pl.BlockSpec((2, blocks, n_grp, depth, width), lambda i: (0, i, 0, 0, 0)),
            pl.BlockSpec(small.shape, lambda i: (0, 0, 0, 0)),
        ],
        out_specs=[
            pl.BlockSpec((rows, hidden), lambda i: (i, 0)),
            pl.BlockSpec((rows, hidden), lambda i: (i, 0)),
            pl.BlockSpec((1, hidden), lambda i: (0, 0)),
            pl.BlockSpec((hidden, upper), lambda i: (0, 0)),
            pl.BlockSpec((1, upper), lambda i: (0, 0)),
        ],
        compiler_params=pltpu.CompilerParams(vmem_limit_bytes=24 * 1024 * 1024),
        name="unpack_grads",
    )(pieces, small)


def gather_kernel(
    n_blk,
    emb_ref, w_left_ref, w_right_ref, ids_ref, target_ref, block_ref, count_ref,
    left_out, right_out, ids_out, target_out, emb_out,
    emb_cols, ids_mine, target_mine, target_in, w_both, w_sem,
    e_send, e_recv, t_send, t_recv, r_send, r_recv, i_send, i_recv,
):
    f32, bf16 = jnp.float32, jnp.bfloat16
    grp, blk = lax.axis_index("grp"), lax.axis_index("blk")
    depth = emb_out.shape[2]
    slots, fold, lanes = target_ref.shape
    before, after = lax.rem(blk + n_blk - 1, n_blk), lax.rem(blk + 1, n_blk)

    def copy(src, dst, send, recv, blk_to):
        return pltpu.make_async_remote_copy(
            src_ref=src, dst_ref=dst, send_sem=send, recv_sem=recv,
            device_id=(grp, blk_to), device_id_type=MESH,
        )

    fetch_right = pltpu.make_async_copy(w_right_ref, w_both.at[1], w_sem.at[1])
    fetch_left = pltpu.make_async_copy(w_left_ref, w_both.at[0], w_sem.at[0])
    fetch_right.start()
    fetch_left.start()
    barrier = pltpu.get_barrier_semaphore()

    def greet(step, carry):
        pl.semaphore_signal(
            barrier, inc=1, device_id=(grp, lax.rem(blk + step, n_blk)), device_id_type=MESH
        )
        return carry
    lax.fori_loop(1, n_blk, greet, 0)

    for to in range(n_blk):
        emb_cols[to] = emb_ref[:, to * depth:(to + 1) * depth]
    ids_mine[...] = jnp.broadcast_to(ids_ref[...], ids_mine.shape)
    ids_out[1] = ids_mine[...]

    pl.semaphore_wait(barrier, n_blk - 1)

    def send_emb(step, carry):
        to = lax.rem(blk + step, n_blk)
        copy(emb_cols.at[to], emb_out.at[blk], e_send.at[step], e_recv.at[step], to).start()
        return carry
    lax.fori_loop(1, n_blk, send_emb, 0)

    def sum_pairs(to):
        for offset in range(3):
            total = jnp.zeros((fold, lanes), f32)
            number = jnp.zeros((8, lanes), f32)
            for slot in range(slots):
                row, col = block_ref[slot, 0], block_ref[slot, 1]
                hit = (row == to) & (col - row == offset - 1) & (slot < count_ref[0, 0])
                weight = jnp.where(hit, 1.0, 0.0).astype(f32)
                total = total + weight * target_ref[slot]
                number = number + weight
            target_mine[to, offset, 0:fold, :] = total
            target_mine[to, offset, fold:fold + 8, :] = number

    def send_targets(step, carry):
        to = lax.rem(blk + step, n_blk)
        sum_pairs(to)
        copy(target_mine.at[to], target_in.at[step], t_send.at[step], t_recv.at[step], to).start()
        return carry
    lax.fori_loop(1, n_blk, send_targets, 0)
    fetch_right.wait()
    right_out[1] = jnp.dot(
        emb_ref[...], w_both[1], preferred_element_type=f32
    ).astype(bf16)
    exchanges = [
        copy(right_out.at[1], right_out.at[2], r_send.at[0], r_recv.at[0], before),
        copy(right_out.at[1], right_out.at[0], r_send.at[1], r_recv.at[1], after),
        copy(ids_mine, ids_out.at[2], i_send.at[0], i_recv.at[0], before),
        copy(ids_mine, ids_out.at[0], i_send.at[1], i_recv.at[1], after),
    ]
    for exchange in exchanges:
        exchange.start()

    fetch_left.wait()
    left_out[...] = jnp.dot(emb_ref[...], w_both[0], preferred_element_type=f32).astype(bf16)
    emb_out[blk] = emb_cols[blk]
    sum_pairs(blk)
    target_out[...] = target_mine[blk]

    def take_targets(step, carry):
        slot = target_in.at[step]
        copy(slot, slot, t_send.at[step], t_recv.at[step], blk).wait_recv()
        target_out[...] += target_in[step]
        return carry
    lax.fori_loop(1, n_blk, take_targets, 0)

    def finish(step, carry):
        slot = emb_out.at[lax.rem(blk + n_blk - step, n_blk)]
        copy(slot, slot, e_send.at[step], e_recv.at[step], blk).wait()
        copy(target_mine.at[0], target_in.at[0], t_send.at[step], t_recv.at[step], blk).wait_send()
        return carry
    lax.fori_loop(1, n_blk, finish, 0)
    for exchange in exchanges:
        exchange.wait()


def gather_panels(n_blk, emb, w_left, w_right, ids, targets, blocks, counts):
    f32, bf16 = jnp.float32, jnp.bfloat16
    panel, wide = emb.shape
    hidden = w_left.shape[1]
    fold, lanes = targets.shape[1:]
    depth = wide // n_blk
    dma = pltpu.SemaphoreType.DMA
    hbm = pl.BlockSpec(memory_space=pl.ANY)
    vmem, smem = pl.BlockSpec(memory_space=pltpu.VMEM), pl.BlockSpec(memory_space=pltpu.SMEM)
    return pl.pallas_call(
        functools.partial(gather_kernel, n_blk),
        out_shape=(
            jax.ShapeDtypeStruct((panel, hidden), bf16),
            jax.ShapeDtypeStruct((3, panel, hidden), bf16),
            jax.ShapeDtypeStruct((3, panel, 128), f32),
            jax.ShapeDtypeStruct((3, fold + 8, lanes), f32),
            jax.ShapeDtypeStruct((n_blk, panel, depth), bf16),
        ),
        in_specs=[vmem, hbm, hbm, vmem, vmem, smem, smem],
        out_specs=[vmem] * 5,
        scratch_shapes=[
            pltpu.VMEM((n_blk, panel, depth), bf16),
            pltpu.VMEM((panel, 128), f32),
            pltpu.VMEM((n_blk, 3, fold + 8, lanes), f32),
            pltpu.VMEM((n_blk, 3, fold + 8, lanes), f32),
            pltpu.VMEM((2, wide, hidden), bf16),
            dma((2,)),
            dma((n_blk,)), dma((n_blk,)), dma((n_blk,)), dma((n_blk,)),
            dma((2,)), dma((2,)), dma((2,)), dma((2,)),
        ],
        compiler_params=pltpu.CompilerParams(
            collective_id=2, has_side_effects=True, vmem_limit_bytes=56 * 1024 * 1024
        ),
        name="gather_panels",
    )(emb, w_left, w_right, ids, targets, blocks, counts)


def local(
    embeddings, cluster_ids, block_list, block_counts, pair_targets,
    w_left, w_right, hidden_bias, w_middle, w_final,
):
    f32, bf16 = jnp.float32, jnp.bfloat16
    n_blk = lax.axis_size("blk")
    n_grp = lax.axis_size("grp")
    emb = embeddings[0]
    panel = emb.shape[0]
    slots = block_list.shape[1]
    hidden = w_left.shape[1]
    upper = w_middle.shape[1]
    fold = panel * panel // 128
    targets = pair_targets[0].reshape(slots, panel, panel // fold, fold)
    targets = targets.transpose(0, 3, 2, 1).reshape(slots, fold, 128)
    ids = cluster_ids[0].astype(f32)
    left, right, col_ids, targets, emb_cols = gather_panels(
        n_blk, emb, w_left, w_right, ids[:, None], targets, block_list[0], block_counts
    )
    left_grad, right_part, sums = pair_grads(
        left, right, hidden_bias, ids[None, :], col_ids, targets, w_middle, w_final
    )
    scale = 1.0 / math.sqrt(n_grp * n_blk * slots * panel)
    grad_local, pieces, small = reduce_grads(
        n_grp, n_blk, scale, left_grad, right_part, emb_cols, w_left, w_right, sums
    )
    grad_left, grad_right, grad_bias, grad_middle, grad_final = unpack_grads(
        scale, pieces, small, hidden, upper
    )
    return grad_local[None], grad_left, grad_right, grad_bias[0], grad_middle, grad_final[0]


def solution(mesh):
    return jax.shard_map(
        local,
        mesh=mesh,
        in_specs=(
            P("grp", "blk", None), P("grp", "blk"), P("grp", "blk", None), P("grp", "blk"),
            P("grp", "blk", None), P(), P(), P(), P(), P(),
        ),
        out_specs=(P("grp", "blk", None), P(), P(), P(), P(), P()),
        check_vma=False,
    )
```

```python
import functools
import math

import jax
import jax.numpy as jnp
from jax import lax
from jax.experimental import pallas as pl
from jax.experimental.pallas import tpu as pltpu
from jax.sharding import PartitionSpec as P

ROWS = 16
COLS = 48
BATCH = 4
MESH = pl.DeviceIdType.MESH


def pair_kernel(
    left_ref, right_ref, bias_ref, row_ids_ref, col_ids_ref, target_ref, middle_ref, final_ref,
    left_out, right_out, sums_out,
    left_half, right_half, right_acc, row_acc, weight_row, target_row,
    half_middle, left_acc, final_acc, middle_acc, slope_ref, act_ref, second_ref,
    half_middle_t,
):
    panel, hidden = left_ref.shape
    span = 3 * panel
    padded = right_acc.shape[0]
    upper = middle_ref.shape[1]
    fold = target_ref.shape[1] - 8
    half_middle[...] = middle_ref[...] * jnp.bfloat16(0.5)
    half_middle_t[...] = half_middle[...].T
    left = left_ref[...].astype(jnp.float32)
    right = right_ref[...].astype(jnp.float32).reshape(span, hidden) + bias_ref[...]
    left_half[...] = 0.5 * left
    right_half[0:span, :] = 0.5 * right
    right_half[span:padded, :] = jnp.zeros((padded - span, hidden), jnp.float32)
    right_acc[...] = jnp.zeros_like(right_acc)
    middle_acc[...] = jnp.zeros_like(middle_acc)
    final_acc[...] = jnp.zeros_like(final_acc)

    row_ids = row_ids_ref[...]
    col_ids = col_ids_ref[...].reshape(span, 128)[:, 0:panel]
    parts, numbers = [], []
    for offset in range(3):
        for lane in range(panel // fold):
            parts.append(target_ref[offset, 0:fold, lane * panel:(lane + 1) * panel])
        numbers.extend([target_ref[offset, fold:fold + 8, 0:panel]] * (panel // 8))
    col_pos = lax.broadcasted_iota(jnp.int32, (span, panel), 0) - panel
    row_pos = lax.broadcasted_iota(jnp.int32, (span, panel), 1)
    used = (col_ids == row_ids) & (col_pos != row_pos)
    counts = jnp.where(used, jnp.concatenate(numbers, axis=0), 0.0) * 16.0
    targets = jnp.where(used, jnp.concatenate(parts, axis=0), 0.0) * 16.0
    tiles = panel // ROWS
    active = jnp.where(counts > 0.0, 1.0, 0.0)
    for tile in range(tiles):
        weight_row[tile, 0:span, :] = counts[:, tile * ROWS:(tile + 1) * ROWS]
        weight_row[tile, span:padded, :] = jnp.zeros((padded - span, ROWS), jnp.float32)
        target_row[tile, 0:span, :] = targets[:, tile * ROWS:(tile + 1) * ROWS]
        target_row[tile, span:padded, :] = jnp.zeros((padded - span, ROWS), jnp.float32)

    where_col = (col_pos + panel).astype(jnp.float32)
    first_map = jnp.where(active > 0.0, where_col, float(padded))
    last_map = jnp.where(active > 0.0, where_col + 1.0, 0.0)
    half_final = 0.5 * final_ref[...]

    for tile in range(tiles):
        lanes = slice(tile * ROWS, (tile + 1) * ROWS)
        first = jnp.min(first_map[:, lanes]).astype(jnp.int32)
        last = jnp.max(last_map[:, lanes]).astype(jnp.int32)
        start = first // 8 * 8
        chunks = jnp.maximum(last - start + COLS - 1, 0) // COLS
        rows = slice(tile * ROWS, (tile + 1) * ROWS)
        row_acc[...] = jnp.zeros_like(row_acc)

        def chunk_step(step, carry):
            first_col = pl.multiple_of(start + step * COLS, 8)
            cols = pl.ds(first_col, COLS)
            weights = weight_row[tile, cols, :]
            goals = target_row[tile, cols, :]

            def open_part(part):
                for row in range(part * BATCH, (part + 1) * BATCH):
                    at = tile * ROWS + row
                    pairs = slice(row * COLS, (row + 1) * COLS)
                    half = (left_half[at:at + 1, :] + right_half[cols, :]).astype(jnp.bfloat16)
                    gate = 1.0 + jnp.tanh(half)
                    act = half * gate
                    slope_ref[pairs, :] = gate * ((half + half) + (1.0 - act))
                    act_ref[pairs, :] = act

            def part_pairs(part):
                return slice(part * BATCH * COLS, (part + 1) * BATCH * COLS)

            open_part(0)
            for part in range(ROWS // BATCH):
                pairs = part_pairs(part)
                upper_half = jnp.dot(
                    act_ref[pairs, :], half_middle[...], preferred_element_type=jnp.float32
                )
                if part + 1 < ROWS // BATCH:
                    open_part(part + 1)
                upper_gate = 1.0 + jnp.tanh(upper_half)
                upper_act = upper_half * upper_gate
                upper_slope = upper_gate * (1.0 + 2.0 * upper_half - upper_act)
                predicted = jnp.sum(upper_act * final_ref[...], axis=1, keepdims=True)
                lanes_of = range(part * BATCH, (part + 1) * BATCH)
                weight = jnp.concatenate([weights[:, a:a + 1] for a in lanes_of], axis=0)
                goal = jnp.concatenate([goals[:, a:a + 1] for a in lanes_of], axis=0)
                pair_slope = weight * predicted - goal
                final_acc[...] += jnp.sum(
                    (upper_act * pair_slope).reshape(BATCH * COLS // 8, 8, upper), axis=0
                )
                second = (pair_slope * half_final * upper_slope).astype(jnp.bfloat16)
                second_ref[pairs, :] = second
                back = jnp.dot(second, half_middle_t[...], preferred_element_type=jnp.float32)
                across = jnp.zeros((COLS, hidden), jnp.float32)
                for row in range(BATCH):
                    index = part * BATCH + row
                    grad = back[row * COLS:(row + 1) * COLS, :]
                    grad = grad * slope_ref[index * COLS:(index + 1) * COLS, :].astype(jnp.float32)
                    across = across + grad
                    row_acc[index] += jnp.sum(grad.reshape(COLS // 8, 8, hidden), axis=0)
                right_acc[cols, :] += across
            middle_acc[...] += lax.dot_general(
                second_ref[...], act_ref[...], (((0,), (0,)), ((), ())),
                preferred_element_type=jnp.float32,
            )
            return carry

        lax.fori_loop(0, chunks, chunk_step, 0)
        left_acc[rows, :] = jnp.sum(row_acc[...], axis=1)
    left_out[...] = left_acc[...].astype(jnp.bfloat16)
    sums_out[0:upper, :] = middle_acc[...].astype(jnp.bfloat16)
    bias_row = jnp.sum(left_acc[...], axis=0, keepdims=True)
    final_row = jnp.sum(final_acc[...], axis=0, keepdims=True)
    final_row = jnp.concatenate([final_row] * (hidden // upper), axis=1)
    row_at = lax.broadcasted_iota(jnp.int32, (16, hidden), 0)
    sums_out[upper:upper + 16, :] = jnp.where(row_at == 0, bias_row, final_row).astype(jnp.bfloat16)
    right_out[...] = right_acc[0:span, :].astype(jnp.bfloat16).reshape(3, panel, hidden)


def pair_grads(left, right, bias, row_ids, col_ids, targets, w_middle, w_final):
    panel, hidden = left.shape
    upper = w_middle.shape[1]
    span = 3 * panel
    padded = span + COLS
    f32 = jnp.float32
    return pl.pallas_call(
        pair_kernel,
        out_shape=(
            jax.ShapeDtypeStruct((panel, hidden), jnp.bfloat16),
            jax.ShapeDtypeStruct((3, panel, hidden), jnp.bfloat16),
            jax.ShapeDtypeStruct((upper + 16, hidden), jnp.bfloat16),
        ),
        in_specs=[pl.BlockSpec(memory_space=pltpu.VMEM)] * 8,
        out_specs=[pl.BlockSpec(memory_space=pltpu.VMEM)] * 3,
        scratch_shapes=[
            pltpu.VMEM((panel, hidden), f32),
            pltpu.VMEM((padded, hidden), f32),
            pltpu.VMEM((padded, hidden), f32),
            pltpu.VMEM((ROWS, 8, hidden), f32),
            pltpu.VMEM((panel // ROWS, padded, ROWS), f32),
            pltpu.VMEM((panel // ROWS, padded, ROWS), f32),
            pltpu.VMEM((hidden, upper), jnp.bfloat16),
            pltpu.VMEM((panel, hidden), f32),
            pltpu.VMEM((8, upper), f32),
            pltpu.VMEM((upper, hidden), f32),
            pltpu.VMEM((ROWS * COLS, hidden), jnp.bfloat16),
            pltpu.VMEM((ROWS * COLS, hidden), jnp.bfloat16),
            pltpu.VMEM((ROWS * COLS, upper), jnp.bfloat16),
            pltpu.VMEM((upper, hidden), jnp.bfloat16),
        ],
        compiler_params=pltpu.CompilerParams(vmem_limit_bytes=32 * 1024 * 1024),
        name="pair_grads",
    )(left, right, bias[None, :], row_ids, col_ids, targets, w_middle, w_final[None, :])


def reduce_kernel(
    n_grp, n_blk, scale,
    left_ref, right_ref, emb_ref, w_left_ref, w_right_ref, sums_ref,
    emb_out, final_out, small_out,
    edge, panels, partial, arrived, mine_g, small, small_in, small_z,
    edge_send, edge_recv, g_send, g_recv, gf_send, gf_recv,
    z_send, z_recv, a_send, a_recv, p_send, p_recv, q_send, q_recv,
    s_send, s_recv, sz_send, sz_recv, sa_send, sa_recv,
):
    f32, bf16 = jnp.float32, jnp.bfloat16
    grp, blk = lax.axis_index("grp"), lax.axis_index("blk")
    chips = n_blk // 2
    chip, core = blk // 2, blk % 2
    panel, hidden = left_ref.shape
    width = hidden // n_grp
    twin = chip * 2 + 1 - core

    def copy(src, dst, send, recv, grp_to, blk_to):
        return pltpu.make_async_remote_copy(
            src_ref=src, dst_ref=dst, send_sem=send, recv_sem=recv,
            device_id=(grp_to, blk_to), device_id_type=MESH,
        )

    def plane(step):
        return lax.rem(chip + step, chips) * 2 + core

    def origin(step):
        return lax.rem(chip + chips - step, chips) * 2 + core

    barrier = pltpu.get_barrier_semaphore()

    def greet_blk(step, carry):
        pl.semaphore_signal(
            barrier, inc=1, device_id=(grp, lax.rem(blk + step, n_blk)), device_id_type=MESH
        )
        return carry

    def greet_grp(step, carry):
        pl.semaphore_signal(
            barrier, inc=1, device_id=(lax.rem(grp + step, n_grp), blk), device_id_type=MESH
        )
        return carry

    lax.fori_loop(1, n_blk, greet_blk, 0)
    lax.fori_loop(1, n_grp, greet_grp, 0)
    panels[0, blk] = left_ref[...]
    share_of = small.shape[1]
    deep = sums_ref.shape[0] // 16
    for tile in range(n_blk * share_of):
        at = small.at[tile // share_of, tile % share_of]
        if tile < deep * (hidden // 128):
            down, across = tile % deep, tile // deep
            at[...] = sums_ref[down * 16:(down + 1) * 16, across * 128:(across + 1) * 128]
        else:
            at[...] = jnp.zeros((16, 128), bf16)
    pl.semaphore_wait(barrier, n_blk - 1 + n_grp - 1)

    to_before = copy(
        right_ref.at[0], edge.at[1], edge_send.at[0], edge_recv.at[1], grp, lax.rem(blk + n_blk - 1, n_blk)
    )
    to_after = copy(
        right_ref.at[2], edge.at[0], edge_send.at[1], edge_recv.at[0], grp, lax.rem(blk + 1, n_blk)
    )
    to_before.start()
    to_after.start()

    def share(half):
        def send(step, carry):
            copy(
                panels.at[half, blk], panels.at[half, blk],
                g_send.at[half, step], g_recv.at[half, step], grp, plane(step),
            ).start()
            return carry
        lax.fori_loop(1, chips, send, 0)
        copy(
            panels.at[half, blk], panels.at[half, blk],
            gf_send.at[half, 0], gf_recv.at[half, 0], grp, twin,
        ).start()

    def forward(half):
        def hand(step, carry):
            slot = panels.at[half, origin(step)]
            copy(slot, slot, g_send.at[half, step], g_recv.at[half, step], grp, plane(step)).wait_recv()
            copy(slot, slot, gf_send.at[half, step], gf_recv.at[half, step], grp, twin).start()
            return carry
        lax.fori_loop(1, chips, hand, 0)

    def multiply(half):
        def take(step, carry):
            slot = panels.at[half, lax.rem(chip + chips - step, chips) * 2 + 1 - core]
            copy(slot, slot, gf_send.at[half, step], gf_recv.at[half, step], grp, twin).wait_recv()
            return carry
        lax.fori_loop(0, chips, take, 0)
        depth = emb_ref.shape[2]
        product = lax.dot_general(
            emb_ref[...].reshape(n_blk * panel, depth), panels[half].reshape(n_blk * panel, hidden),
            (((0,), (0,)), ((), ())), preferred_element_type=f32,
        )
        for part in range(n_grp):
            partial[half, part] = product[:, part * width:(part + 1) * width].astype(bf16)

        def send(step, carry):
            to = lax.rem(grp + step, n_grp)
            copy(
                partial.at[half, to], arrived.at[half, step],
                z_send.at[half, step], z_recv.at[half, step], to, blk,
            ).start()
            return carry
        lax.fori_loop(1, n_grp, send, 0)

    def spread(half, part):
        slot = final_out.at[half, blk, part]

        def send(step, carry):
            copy(
                slot, slot, p_send.at[half, part, step], p_recv.at[half, part, step], grp, plane(step)
            ).start()
            return carry
        lax.fori_loop(1, chips, send, 0)
        copy(slot, slot, q_send.at[half, part, 0], q_recv.at[half, part, 0], grp, twin).start()

    def combine(half):
        total = partial[half, grp].astype(f32)
        for step in range(1, n_grp):
            slot = arrived.at[half, step]
            copy(slot, slot, z_send.at[half, step], z_recv.at[half, step], grp, blk).wait_recv()
            total = total + arrived[half, step].astype(f32)
        final_out[half, blk, grp] = (total * scale).astype(bf16)
        slot = final_out.at[half, blk, grp]

        def send(step, carry):
            copy(
                slot, slot, a_send.at[half, step], a_recv.at[half, step],
                lax.rem(grp + step, n_grp), blk,
            ).start()
            return carry
        lax.fori_loop(1, n_grp, send, 0)
        spread(half, grp)

    share(0)

    def small_start(step, carry):
        to = lax.rem(blk + step, n_blk)
        copy(small.at[to], small_in.at[step], s_send.at[step], s_recv.at[step], grp, to).start()
        return carry
    lax.fori_loop(1, n_blk, small_start, 0)
    to_before.wait_recv()
    to_after.wait_recv()
    right = right_ref[1].astype(f32)
    right = right + jnp.where(blk > 0, edge[0].astype(f32), 0.0)
    right = right + jnp.where(blk < n_blk - 1, edge[1].astype(f32), 0.0)
    panels[1, blk] = right.astype(bf16)
    mine_g[...] = right.astype(bf16)
    share(1)
    forward(0)
    multiply(0)
    forward(1)
    multiply(1)
    combine(0)
    small_sum = small[blk].astype(f32)
    for step in range(1, n_blk):
        slot = small_in.at[step]
        copy(slot, slot, s_send.at[step], s_recv.at[step], grp, blk).wait_recv()
        small_sum = small_sum + small_in[step].astype(f32)
    small_z[grp] = small_sum.astype(bf16)

    def small_across(step, carry):
        slot = small_z.at[grp]
        copy(slot, slot, sz_send.at[step], sz_recv.at[step], lax.rem(grp + step, n_grp), blk).start()
        return carry
    lax.fori_loop(1, n_grp, small_across, 0)

    combine(1)
    for half in range(2):
        def pass_on(step, carry):
            part = lax.rem(grp + n_grp - step, n_grp)
            slot = final_out.at[half, blk, part]
            copy(slot, slot, a_send.at[half, step], a_recv.at[half, step], grp, blk).wait_recv()
            spread(half, part)
            return carry
        lax.fori_loop(1, n_grp, pass_on, 0)

    def small_take(step, carry):
        slot = small_z.at[lax.rem(grp + n_grp - step, n_grp)]
        copy(slot, slot, sz_send.at[step], sz_recv.at[step], grp, blk).wait_recv()
        return carry
    lax.fori_loop(1, n_grp, small_take, 0)
    small_total = small_z[0].astype(f32)
    for group in range(1, n_grp):
        small_total = small_total + small_z[group].astype(f32)
    small_out[blk] = small_total.astype(bf16)

    def small_spread(step, carry):
        slot = small_out.at[blk]
        copy(
            slot, slot, sa_send.at[step], sa_recv.at[step], grp, lax.rem(blk + step, n_blk)
        ).start()
        return carry
    lax.fori_loop(1, n_blk, small_spread, 0)
    def hand_on(index, carry):
        half, rest = index // n_grp, lax.rem(index, n_grp)
        part = lax.rem(grp + n_grp - rest, n_grp)

        def hand(step, inner):
            slot = final_out.at[half, origin(step), part]
            copy(
                slot, slot, p_send.at[half, part, step], p_recv.at[half, part, step], grp, plane(step)
            ).wait_recv()
            copy(
                slot, slot, q_send.at[half, part, step], q_recv.at[half, part, step], grp, twin
            ).start()
            return inner
        return lax.fori_loop(1, chips, hand, carry)
    emb_out[...] = lax.dot_general(
        left_ref[...], w_left_ref[...], (((1,), (1,)), ((), ())), preferred_element_type=f32
    )
    emb_out[...] += lax.dot_general(
        mine_g[...], w_right_ref[...], (((1,), (1,)), ((), ())), preferred_element_type=f32
    )
    lax.fori_loop(0, 2 * n_grp, hand_on, 0)

    def finish(index, carry):
        half, part = index // n_grp, lax.rem(index, n_grp)

        def end(step, inner):
            slot = final_out.at[half, lax.rem(chip + chips - step, chips) * 2 + 1 - core, part]
            copy(
                slot, slot, q_send.at[half, part, step], q_recv.at[half, part, step], grp, twin
            ).wait()
            return inner
        lax.fori_loop(0, chips, end, 0)

        def sent(step, inner):
            slot = final_out.at[half, blk, part]
            copy(
                slot, slot, p_send.at[half, part, step], p_recv.at[half, part, step], grp, plane(step)
            ).wait_send()
            return inner
        return lax.fori_loop(1, chips, sent, carry)
    lax.fori_loop(0, 2 * n_grp, finish, 0)

    to_before.wait_send()
    to_after.wait_send()

    def small_end(step, carry):
        slot = small_out.at[lax.rem(blk + n_blk - step, n_blk)]
        copy(slot, slot, sa_send.at[step], sa_recv.at[step], grp, blk).wait()
        copy(small.at[0], small_in.at[0], s_send.at[step], s_recv.at[step], grp, blk).wait_send()
        return carry
    lax.fori_loop(1, n_blk, small_end, 0)

    def small_end_z(step, carry):
        slot = small_z.at[0]
        copy(slot, slot, sz_send.at[step], sz_recv.at[step], grp, blk).wait_send()
        return carry
    lax.fori_loop(1, n_grp, small_end_z, 0)
    for half in range(2):
        def g_done(step, carry):
            slot = panels.at[half, blk]
            copy(slot, slot, g_send.at[half, step], g_recv.at[half, step], grp, plane(step)).wait_send()
            return carry
        lax.fori_loop(1, chips, g_done, 0)

        def gf_done(step, carry):
            slot = panels.at[half, blk]
            copy(slot, slot, gf_send.at[half, step], gf_recv.at[half, step], grp, twin).wait_send()
            return carry
        lax.fori_loop(0, chips, gf_done, 0)

        def z_done(step, carry):
            slot = partial.at[half, 0]
            copy(slot, slot, z_send.at[half, step], z_recv.at[half, step], grp, blk).wait_send()
            slot = final_out.at[half, blk, 0]
            copy(slot, slot, a_send.at[half, step], a_recv.at[half, step], grp, blk).wait_send()
            return carry
        lax.fori_loop(1, n_grp, z_done, 0)


def reduce_grads(n_grp, n_blk, scale, left_grad, right_part, emb_cols, w_left, w_right, sums):
    panel, hidden = left_grad.shape
    depth = emb_cols.shape[2]
    wide = w_left.shape[0]
    chips = n_blk // 2
    width = hidden // n_grp
    share_of = -(-(sums.shape[0] // 16 * (hidden // 128)) // n_blk)
    bf16 = jnp.bfloat16
    dma = pltpu.SemaphoreType.DMA
    return pl.pallas_call(
        functools.partial(reduce_kernel, n_grp, n_blk, scale),
        out_shape=(
            jax.ShapeDtypeStruct((panel, wide), jnp.float32),
            jax.ShapeDtypeStruct((2, n_blk, n_grp, depth, width), bf16),
            jax.ShapeDtypeStruct((n_blk, share_of, 16, 128), bf16),
        ),
        in_specs=[pl.BlockSpec(memory_space=pltpu.VMEM)] * 6,
        out_specs=[pl.BlockSpec(memory_space=pltpu.VMEM)] * 3,
        scratch_shapes=[
            pltpu.VMEM((2, panel, hidden), bf16),
            pltpu.VMEM((2, n_blk, panel, hidden), bf16),
            pltpu.VMEM((2, n_grp, depth, width), bf16),
            pltpu.VMEM((2, n_grp, depth, width), bf16),
            pltpu.VMEM((panel, hidden), bf16),
            pltpu.VMEM((n_blk, share_of, 16, 128), bf16),
            pltpu.VMEM((n_blk, share_of, 16, 128), bf16),
            pltpu.VMEM((n_grp, share_of, 16, 128), bf16),
            dma((2,)), dma((2,)),
            dma((2, chips)), dma((2, chips)), dma((2, chips)), dma((2, chips)),
            dma((2, n_grp)), dma((2, n_grp)), dma((2, n_grp)), dma((2, n_grp)),
            dma((2, n_grp, chips)), dma((2, n_grp, chips)),
            dma((2, n_grp, chips)), dma((2, n_grp, chips)),
            dma((n_blk,)), dma((n_blk,)), dma((n_grp,)), dma((n_grp,)), dma((n_blk,)), dma((n_blk,)),
        ],
        compiler_params=pltpu.CompilerParams(
            collective_id=1, has_side_effects=True, vmem_limit_bytes=40 * 1024 * 1024
        ),
        name="reduce_grads",
    )(left_grad, right_part, emb_cols, w_left, w_right, sums)


def unpack_kernel(scale, pieces_ref, small_ref, left_out, right_out, bias_out, middle_out, final_out):
    f32 = jnp.float32
    blocks, n_grp, depth, width = pieces_ref.shape[1:]
    for half, out in enumerate((left_out, right_out)):
        for block in range(blocks):
            for part in range(n_grp):
                out[block * depth:(block + 1) * depth, part * width:(part + 1) * width] = (
                    pieces_ref[half, block, part].astype(f32)
                )

    @pl.when(pl.program_id(0) == 0)
    def _():
        share_of = small_ref.shape[1]
        upper = middle_out.shape[1]
        deep = upper // 16 + 1

        def tile(down, across):
            at = across * deep + down
            return small_ref[at // share_of, at % share_of].astype(f32) * scale

        for across in range(middle_out.shape[0] // 128):
            lanes = slice(across * 128, (across + 1) * 128)
            rows = jnp.concatenate([tile(down, across) for down in range(deep - 1)], axis=0)
            middle_out[lanes, :] = rows.T
            bias_out[:, lanes] = tile(deep - 1, across)[0:1, :]
        final_out[...] = tile(deep - 1, 0)[1:2, 0:upper]


def unpack_grads(scale, pieces, small, hidden, upper):
    _, n_blk, n_grp, depth, width = pieces.shape
    steps = math.gcd(n_blk, 4)
    blocks = n_blk // steps
    f32 = jnp.float32
    rows = blocks * depth
    return pl.pallas_call(
        functools.partial(unpack_kernel, scale),
        grid=(steps,),
        out_shape=(
            jax.ShapeDtypeStruct((n_blk * depth, hidden), f32),
            jax.ShapeDtypeStruct((n_blk * depth, hidden), f32),
            jax.ShapeDtypeStruct((1, hidden), f32),
            jax.ShapeDtypeStruct((hidden, upper), f32),
            jax.ShapeDtypeStruct((1, upper), f32),
        ),
        in_specs=[
            pl.BlockSpec((2, blocks, n_grp, depth, width), lambda i: (0, i, 0, 0, 0)),
            pl.BlockSpec(small.shape, lambda i: (0, 0, 0, 0)),
        ],
        out_specs=[
            pl.BlockSpec((rows, hidden), lambda i: (i, 0)),
            pl.BlockSpec((rows, hidden), lambda i: (i, 0)),
            pl.BlockSpec((1, hidden), lambda i: (0, 0)),
            pl.BlockSpec((hidden, upper), lambda i: (0, 0)),
            pl.BlockSpec((1, upper), lambda i: (0, 0)),
        ],
        compiler_params=pltpu.CompilerParams(vmem_limit_bytes=24 * 1024 * 1024),
        name="unpack_grads",
    )(pieces, small)


def gather_kernel(
    n_blk,
    emb_ref, w_left_ref, w_right_ref, ids_ref, target_ref, block_ref, count_ref,
    left_out, right_out, ids_out, target_out, emb_out,
    emb_cols, ids_mine, target_mine, target_in, w_both, w_sem,
    e_send, e_recv, t_send, t_recv, r_send, r_recv, i_send, i_recv,
):
    f32, bf16 = jnp.float32, jnp.bfloat16
    grp, blk = lax.axis_index("grp"), lax.axis_index("blk")
    depth = emb_out.shape[2]
    slots, fold, lanes = target_ref.shape
    before, after = lax.rem(blk + n_blk - 1, n_blk), lax.rem(blk + 1, n_blk)

    def copy(src, dst, send, recv, blk_to):
        return pltpu.make_async_remote_copy(
            src_ref=src, dst_ref=dst, send_sem=send, recv_sem=recv,
            device_id=(grp, blk_to), device_id_type=MESH,
        )

    fetch_right = pltpu.make_async_copy(w_right_ref, w_both.at[1], w_sem.at[1])
    fetch_left = pltpu.make_async_copy(w_left_ref, w_both.at[0], w_sem.at[0])
    fetch_right.start()
    fetch_left.start()
    barrier = pltpu.get_barrier_semaphore()

    def greet(step, carry):
        pl.semaphore_signal(
            barrier, inc=1, device_id=(grp, lax.rem(blk + step, n_blk)), device_id_type=MESH
        )
        return carry
    lax.fori_loop(1, n_blk, greet, 0)

    for to in range(n_blk):
        emb_cols[to] = emb_ref[:, to * depth:(to + 1) * depth]
    ids_mine[...] = jnp.broadcast_to(ids_ref[...], ids_mine.shape)
    ids_out[1] = ids_mine[...]

    pl.semaphore_wait(barrier, n_blk - 1)

    def send_emb(step, carry):
        to = lax.rem(blk + step, n_blk)
        copy(emb_cols.at[to], emb_out.at[blk], e_send.at[step], e_recv.at[step], to).start()
        return carry
    lax.fori_loop(1, n_blk, send_emb, 0)

    def sum_pairs(to):
        for offset in range(3):
            total = jnp.zeros((fold, lanes), f32)
            number = jnp.zeros((8, lanes), f32)
            for slot in range(slots):
                row, col = block_ref[slot, 0], block_ref[slot, 1]
                hit = (row == to) & (col - row == offset - 1) & (slot < count_ref[0, 0])
                weight = jnp.where(hit, 1.0, 0.0).astype(f32)
                total = total + weight * target_ref[slot]
                number = number + weight
            target_mine[to, offset, 0:fold, :] = total
            target_mine[to, offset, fold:fold + 8, :] = number

    def send_targets(step, carry):
        to = lax.rem(blk + step, n_blk)
        sum_pairs(to)
        copy(target_mine.at[to], target_in.at[step], t_send.at[step], t_recv.at[step], to).start()
        return carry
    lax.fori_loop(1, n_blk, send_targets, 0)
    fetch_right.wait()
    right_out[1] = jnp.dot(
        emb_ref[...], w_both[1], preferred_element_type=f32
    ).astype(bf16)
    exchanges = [
        copy(right_out.at[1], right_out.at[2], r_send.at[0], r_recv.at[0], before),
        copy(right_out.at[1], right_out.at[0], r_send.at[1], r_recv.at[1], after),
        copy(ids_mine, ids_out.at[2], i_send.at[0], i_recv.at[0], before),
        copy(ids_mine, ids_out.at[0], i_send.at[1], i_recv.at[1], after),
    ]
    for exchange in exchanges:
        exchange.start()

    fetch_left.wait()
    left_out[...] = jnp.dot(emb_ref[...], w_both[0], preferred_element_type=f32).astype(bf16)
    emb_out[blk] = emb_cols[blk]
    sum_pairs(blk)
    target_out[...] = target_mine[blk]

    def take_targets(step, carry):
        slot = target_in.at[step]
        copy(slot, slot, t_send.at[step], t_recv.at[step], blk).wait_recv()
        target_out[...] += target_in[step]
        return carry
    lax.fori_loop(1, n_blk, take_targets, 0)

    def finish(step, carry):
        slot = emb_out.at[lax.rem(blk + n_blk - step, n_blk)]
        copy(slot, slot, e_send.at[step], e_recv.at[step], blk).wait()
        copy(target_mine.at[0], target_in.at[0], t_send.at[step], t_recv.at[step], blk).wait_send()
        return carry
    lax.fori_loop(1, n_blk, finish, 0)
    for exchange in exchanges:
        exchange.wait()


def gather_panels(n_blk, emb, w_left, w_right, ids, targets, blocks, counts):
    f32, bf16 = jnp.float32, jnp.bfloat16
    panel, wide = emb.shape
    hidden = w_left.shape[1]
    fold, lanes = targets.shape[1:]
    depth = wide // n_blk
    dma = pltpu.SemaphoreType.DMA
    hbm = pl.BlockSpec(memory_space=pl.ANY)
    vmem, smem = pl.BlockSpec(memory_space=pltpu.VMEM), pl.BlockSpec(memory_space=pltpu.SMEM)
    return pl.pallas_call(
        functools.partial(gather_kernel, n_blk),
        out_shape=(
            jax.ShapeDtypeStruct((panel, hidden), bf16),
            jax.ShapeDtypeStruct((3, panel, hidden), bf16),
            jax.ShapeDtypeStruct((3, panel, 128), f32),
            jax.ShapeDtypeStruct((3, fold + 8, lanes), f32),
            jax.ShapeDtypeStruct((n_blk, panel, depth), bf16),
        ),
        in_specs=[vmem, hbm, hbm, vmem, vmem, smem, smem],
        out_specs=[vmem] * 5,
        scratch_shapes=[
            pltpu.VMEM((n_blk, panel, depth), bf16),
            pltpu.VMEM((panel, 128), f32),
            pltpu.VMEM((n_blk, 3, fold + 8, lanes), f32),
            pltpu.VMEM((n_blk, 3, fold + 8, lanes), f32),
            pltpu.VMEM((2, wide, hidden), bf16),
            dma((2,)),
            dma((n_blk,)), dma((n_blk,)), dma((n_blk,)), dma((n_blk,)),
            dma((2,)), dma((2,)), dma((2,)), dma((2,)),
        ],
        compiler_params=pltpu.CompilerParams(
            collective_id=2, has_side_effects=True, vmem_limit_bytes=32 * 1024 * 1024
        ),
        name="gather_panels",
    )(emb, w_left, w_right, ids, targets, blocks, counts)


def local(
    embeddings, cluster_ids, block_list, block_counts, pair_targets,
    w_left, w_right, hidden_bias, w_middle, w_final,
):
    f32, bf16 = jnp.float32, jnp.bfloat16
    n_blk = lax.axis_size("blk")
    n_grp = lax.axis_size("grp")
    emb = embeddings[0]
    panel = emb.shape[0]
    slots = block_list.shape[1]
    hidden = w_left.shape[1]
    upper = w_middle.shape[1]
    fold = panel * panel // 128
    targets = pair_targets[0].reshape(slots, panel, panel // fold, fold)
    targets = targets.transpose(0, 3, 2, 1).reshape(slots, fold, 128)
    ids = cluster_ids[0].astype(f32)
    left, right, col_ids, targets, emb_cols = gather_panels(
        n_blk, emb, w_left, w_right, ids[:, None], targets, block_list[0], block_counts
    )
    left_grad, right_part, sums = pair_grads(
        left, right, hidden_bias, ids[None, :], col_ids, targets, w_middle, w_final
    )
    scale = 1.0 / math.sqrt(n_grp * n_blk * slots * panel)
    grad_local, pieces, small = reduce_grads(
        n_grp, n_blk, scale, left_grad, right_part, emb_cols, w_left, w_right, sums
    )
    grad_left, grad_right, grad_bias, grad_middle, grad_final = unpack_grads(
        scale, pieces, small, hidden, upper
    )
    return grad_local[None], grad_left, grad_right, grad_bias[0], grad_middle, grad_final[0]


def solution(mesh):
    return jax.shard_map(
        local,
        mesh=mesh,
        in_specs=(
            P("grp", "blk", None), P("grp", "blk"), P("grp", "blk", None), P("grp", "blk"),
            P("grp", "blk", None), P(), P(), P(), P(), P(),
        ),
        out_specs=(P("grp", "blk", None), P(), P(), P(), P(), P()),
        check_vma=False,
    )
```

```python
import functools
import math

import jax
import jax.numpy as jnp
from jax import lax
from jax.experimental import pallas as pl
from jax.experimental.pallas import tpu as pltpu
from jax.sharding import PartitionSpec as P

ROWS = 16
COLS = 48
BATCH = 4
MESH = pl.DeviceIdType.MESH


def pair_kernel(
    left_ref, right_ref, bias_ref, row_ids_ref, col_ids_ref, target_ref, middle_ref, final_ref,
    left_out, right_out, sums_out,
    left_half, right_half, right_acc, row_acc, coded, spread, ones,
    half_middle, left_acc, final_acc, middle_acc, slope_ref, act_ref, second_ref,
    half_middle_t,
):
    panel, hidden = left_ref.shape
    span = 3 * panel
    padded = right_acc.shape[0]
    upper = middle_ref.shape[1]
    fold = target_ref.shape[1] - 8
    half_middle[...] = middle_ref[...] * jnp.bfloat16(0.5)
    half_middle_t[...] = half_middle[...].T
    left = left_ref[...].astype(jnp.float32)
    right = right_ref[...].astype(jnp.float32).reshape(span, hidden) + bias_ref[...]
    left_half[...] = 0.5 * left
    right_half[0:span, :] = 0.5 * right
    right_half[span:padded, :] = jnp.zeros((padded - span, hidden), jnp.float32)
    right_acc[...] = jnp.zeros_like(right_acc)
    middle_acc[...] = jnp.zeros_like(middle_acc)
    final_acc[...] = jnp.zeros_like(final_acc)

    row_ids = row_ids_ref[...]
    col_ids = col_ids_ref[...].reshape(span, 128)[:, 0:panel]
    parts, numbers = [], []
    for offset in range(3):
        for lane in range(panel // fold):
            parts.append(target_ref[offset, 0:fold, lane * panel:(lane + 1) * panel])
        numbers.extend([target_ref[offset, fold:fold + 8, 0:panel]] * (panel // 8))
    col_pos = lax.broadcasted_iota(jnp.int32, (span, panel), 0) - panel
    row_pos = lax.broadcasted_iota(jnp.int32, (span, panel), 1)
    used = (col_ids == row_ids) & (col_pos != row_pos)
    counts = jnp.where(used, jnp.concatenate(numbers, axis=0), 0.0) * 16.0
    targets = jnp.where(used, jnp.concatenate(parts, axis=0), 0.0) * 16.0
    tiles = panel // ROWS
    active = jnp.where(counts > 0.0, 1.0, 0.0)
    for tile in range(tiles):
        lanes = slice(tile * ROWS, (tile + 1) * ROWS)
        goal = targets[:, lanes]
        goal_high = goal.astype(jnp.bfloat16).astype(jnp.float32)
        coded[tile, 0:span, :] = jnp.concatenate(
            [counts[:, lanes], goal_high, goal - goal_high,
             jnp.zeros((span, 128 - 3 * ROWS), jnp.float32)], axis=1
        )
        coded[tile, span:padded, :] = jnp.zeros((padded - span, 128), jnp.float32)
    spread_row = lax.broadcasted_iota(jnp.int32, (128, 2 * upper), 0)
    spread_col = lax.broadcasted_iota(jnp.int32, (128, 2 * upper), 1)
    spread[...] = jnp.where((spread_row < ROWS) == (spread_col < upper), 1.0, 0.0).astype(jnp.bfloat16)
    ones[...] = jnp.ones(ones.shape, jnp.bfloat16)

    where_col = (col_pos + panel).astype(jnp.float32)
    first_map = jnp.where(active > 0.0, where_col, float(padded))
    last_map = jnp.where(active > 0.0, where_col + 1.0, 0.0)
    half_final = 0.5 * final_ref[...]

    for tile in range(tiles):
        lanes = slice(tile * ROWS, (tile + 1) * ROWS)
        first = jnp.min(first_map[:, lanes]).astype(jnp.int32)
        last = jnp.max(last_map[:, lanes]).astype(jnp.int32)
        start = first // 8 * 8
        chunks = jnp.maximum(last - start + COLS - 1, 0) // COLS
        rows = slice(tile * ROWS, (tile + 1) * ROWS)
        row_acc[...] = jnp.zeros_like(row_acc)

        def chunk_step(step, carry):
            first_col = pl.multiple_of(start + step * COLS, 8)
            cols = pl.ds(first_col, COLS)
            code = coded[tile, cols, :]
            code_row = lax.broadcasted_iota(jnp.int32, (COLS, 128), 1) % ROWS

            def open_part(part):
                for row in range(part * BATCH, (part + 1) * BATCH):
                    at = tile * ROWS + row
                    pairs = slice(row * COLS, (row + 1) * COLS)
                    half = (left_half[at:at + 1, :] + right_half[cols, :]).astype(jnp.bfloat16)
                    gate = 1.0 + jnp.tanh(half)
                    act = half * gate
                    slope_ref[pairs, :] = gate * ((half + half) + (1.0 - act))
                    act_ref[pairs, :] = act

            def part_pairs(part):
                return slice(part * BATCH * COLS, (part + 1) * BATCH * COLS)

            open_part(0)
            for part in range(ROWS // BATCH):
                pairs = part_pairs(part)
                upper_half = jnp.dot(
                    act_ref[pairs, :], half_middle[...], preferred_element_type=jnp.float32
                )
                if part + 1 < ROWS // BATCH:
                    open_part(part + 1)
                upper_gate = 1.0 + jnp.tanh(upper_half)
                upper_act = upper_half * upper_gate
                upper_slope = upper_gate * (1.0 + 2.0 * upper_half - upper_act)
                terms = upper_act * final_ref[...]
                terms_high = terms.astype(jnp.bfloat16)
                terms_low = (terms - terms_high.astype(jnp.float32)).astype(jnp.bfloat16)
                predicted = jnp.dot(
                    jnp.concatenate([terms_high, terms_low], axis=1), ones[...],
                    preferred_element_type=jnp.float32,
                )
                picked = jnp.concatenate(
                    [jnp.where(code_row == a, code, 0.0).astype(jnp.bfloat16)
                     for a in range(part * BATCH, (part + 1) * BATCH)], axis=0
                )
                both = jnp.dot(picked, spread[...], preferred_element_type=jnp.float32)
                pair_slope = both[:, 0:upper] * predicted - both[:, upper:2 * upper]
                final_acc[...] += jnp.sum(
                    (upper_act * pair_slope).reshape(BATCH * COLS // 8, 8, upper), axis=0
                )
                second = (pair_slope * half_final * upper_slope).astype(jnp.bfloat16)
                second_ref[pairs, :] = second
                back = jnp.dot(second, half_middle_t[...], preferred_element_type=jnp.float32)
                across = jnp.zeros((COLS, hidden), jnp.float32)
                for row in range(BATCH):
                    index = part * BATCH + row
                    grad = back[row * COLS:(row + 1) * COLS, :]
                    grad = grad * slope_ref[index * COLS:(index + 1) * COLS, :].astype(jnp.float32)
                    across = across + grad
                    row_acc[index] += jnp.sum(grad.reshape(COLS // 8, 8, hidden), axis=0)
                right_acc[cols, :] += across
            middle_acc[...] += lax.dot_general(
                second_ref[...], act_ref[...], (((0,), (0,)), ((), ())),
                preferred_element_type=jnp.float32,
            )
            return carry

        lax.fori_loop(0, chunks, chunk_step, 0)
        left_acc[rows, :] = jnp.sum(row_acc[...], axis=1)
    left_out[...] = left_acc[...].astype(jnp.bfloat16)
    sums_out[0:upper, :] = middle_acc[...].astype(jnp.bfloat16)
    bias_row = jnp.sum(left_acc[...], axis=0, keepdims=True)
    final_row = jnp.sum(final_acc[...], axis=0, keepdims=True)
    final_row = jnp.concatenate([final_row] * (hidden // upper), axis=1)
    row_at = lax.broadcasted_iota(jnp.int32, (16, hidden), 0)
    sums_out[upper:upper + 16, :] = jnp.where(row_at == 0, bias_row, final_row).astype(jnp.bfloat16)
    right_out[...] = right_acc[0:span, :].astype(jnp.bfloat16).reshape(3, panel, hidden)


def pair_grads(left, right, bias, row_ids, col_ids, targets, w_middle, w_final):
    panel, hidden = left.shape
    upper = w_middle.shape[1]
    span = 3 * panel
    padded = span + COLS
    f32 = jnp.float32
    return pl.pallas_call(
        pair_kernel,
        out_shape=(
            jax.ShapeDtypeStruct((panel, hidden), jnp.bfloat16),
            jax.ShapeDtypeStruct((3, panel, hidden), jnp.bfloat16),
            jax.ShapeDtypeStruct((upper + 16, hidden), jnp.bfloat16),
        ),
        in_specs=[pl.BlockSpec(memory_space=pltpu.VMEM)] * 8,
        out_specs=[pl.BlockSpec(memory_space=pltpu.VMEM)] * 3,
        scratch_shapes=[
            pltpu.VMEM((panel, hidden), f32),
            pltpu.VMEM((padded, hidden), f32),
            pltpu.VMEM((padded, hidden), f32),
            pltpu.VMEM((ROWS, 8, hidden), f32),
            pltpu.VMEM((panel // ROWS, padded, 128), f32),
            pltpu.VMEM((128, 2 * upper), jnp.bfloat16),
            pltpu.VMEM((2 * upper, upper), jnp.bfloat16),
            pltpu.VMEM((hidden, upper), jnp.bfloat16),
            pltpu.VMEM((panel, hidden), f32),
            pltpu.VMEM((8, upper), f32),
            pltpu.VMEM((upper, hidden), f32),
            pltpu.VMEM((ROWS * COLS, hidden), jnp.bfloat16),
            pltpu.VMEM((ROWS * COLS, hidden), jnp.bfloat16),
            pltpu.VMEM((ROWS * COLS, upper), jnp.bfloat16),
            pltpu.VMEM((upper, hidden), jnp.bfloat16),
        ],
        compiler_params=pltpu.CompilerParams(vmem_limit_bytes=32 * 1024 * 1024),
        name="pair_grads",
    )(left, right, bias[None, :], row_ids, col_ids, targets, w_middle, w_final[None, :])


def reduce_kernel(
    n_grp, n_blk, scale,
    left_ref, right_ref, emb_ref, w_left_ref, w_right_ref, sums_ref,
    emb_out, final_out, small_out,
    edge, panels, partial, arrived, mine_g, small, small_in, small_z,
    edge_send, edge_recv, g_send, g_recv, gf_send, gf_recv,
    z_send, z_recv, a_send, a_recv, p_send, p_recv, q_send, q_recv,
    s_send, s_recv, sz_send, sz_recv, sa_send, sa_recv,
):
    f32, bf16 = jnp.float32, jnp.bfloat16
    grp, blk = lax.axis_index("grp"), lax.axis_index("blk")
    chips = n_blk // 2
    chip, core = blk // 2, blk % 2
    panel, hidden = left_ref.shape
    width = hidden // n_grp
    twin = chip * 2 + 1 - core

    def copy(src, dst, send, recv, grp_to, blk_to):
        return pltpu.make_async_remote_copy(
            src_ref=src, dst_ref=dst, send_sem=send, recv_sem=recv,
            device_id=(grp_to, blk_to), device_id_type=MESH,
        )

    def plane(step):
        return lax.rem(chip + step, chips) * 2 + core

    def origin(step):
        return lax.rem(chip + chips - step, chips) * 2 + core

    barrier = pltpu.get_barrier_semaphore()

    def greet_blk(step, carry):
        pl.semaphore_signal(
            barrier, inc=1, device_id=(grp, lax.rem(blk + step, n_blk)), device_id_type=MESH
        )
        return carry

    def greet_grp(step, carry):
        pl.semaphore_signal(
            barrier, inc=1, device_id=(lax.rem(grp + step, n_grp), blk), device_id_type=MESH
        )
        return carry

    lax.fori_loop(1, n_blk, greet_blk, 0)
    lax.fori_loop(1, n_grp, greet_grp, 0)
    panels[0, blk] = left_ref[...]
    share_of = small.shape[1]
    deep = sums_ref.shape[0] // 16
    for tile in range(n_blk * share_of):
        at = small.at[tile // share_of, tile % share_of]
        if tile < deep * (hidden // 128):
            down, across = tile % deep, tile // deep
            at[...] = sums_ref[down * 16:(down + 1) * 16, across * 128:(across + 1) * 128]
        else:
            at[...] = jnp.zeros((16, 128), bf16)
    pl.semaphore_wait(barrier, n_blk - 1 + n_grp - 1)

    to_before = copy(
        right_ref.at[0], edge.at[1], edge_send.at[0], edge_recv.at[1], grp, lax.rem(blk + n_blk - 1, n_blk)
    )
    to_after = copy(
        right_ref.at[2], edge.at[0], edge_send.at[1], edge_recv.at[0], grp, lax.rem(blk + 1, n_blk)
    )
    to_before.start()
    to_after.start()

    def share(half):
        def send(step, carry):
            copy(
                panels.at[half, blk], panels.at[half, blk],
                g_send.at[half, step], g_recv.at[half, step], grp, plane(step),
            ).start()
            return carry
        lax.fori_loop(1, chips, send, 0)
        copy(
            panels.at[half, blk], panels.at[half, blk],
            gf_send.at[half, 0], gf_recv.at[half, 0], grp, twin,
        ).start()

    def forward(half):
        def hand(step, carry):
            slot = panels.at[half, origin(step)]
            copy(slot, slot, g_send.at[half, step], g_recv.at[half, step], grp, plane(step)).wait_recv()
            copy(slot, slot, gf_send.at[half, step], gf_recv.at[half, step], grp, twin).start()
            return carry
        lax.fori_loop(1, chips, hand, 0)

    def multiply(half):
        def take(step, carry):
            slot = panels.at[half, lax.rem(chip + chips - step, chips) * 2 + 1 - core]
            copy(slot, slot, gf_send.at[half, step], gf_recv.at[half, step], grp, twin).wait_recv()
            return carry
        lax.fori_loop(0, chips, take, 0)
        depth = emb_ref.shape[2]
        product = lax.dot_general(
            emb_ref[...].reshape(n_blk * panel, depth), panels[half].reshape(n_blk * panel, hidden),
            (((0,), (0,)), ((), ())), preferred_element_type=f32,
        )
        for part in range(n_grp):
            partial[half, part] = product[:, part * width:(part + 1) * width].astype(bf16)

        def send(step, carry):
            to = lax.rem(grp + step, n_grp)
            copy(
                partial.at[half, to], arrived.at[half, step],
                z_send.at[half, step], z_recv.at[half, step], to, blk,
            ).start()
            return carry
        lax.fori_loop(1, n_grp, send, 0)

    def spread(half, part):
        slot = final_out.at[half, blk, part]

        def send(step, carry):
            copy(
                slot, slot, p_send.at[half, part, step], p_recv.at[half, part, step], grp, plane(step)
            ).start()
            return carry
        lax.fori_loop(1, chips, send, 0)
        copy(slot, slot, q_send.at[half, part, 0], q_recv.at[half, part, 0], grp, twin).start()

    def combine(half):
        total = partial[half, grp].astype(f32)
        for step in range(1, n_grp):
            slot = arrived.at[half, step]
            copy(slot, slot, z_send.at[half, step], z_recv.at[half, step], grp, blk).wait_recv()
            total = total + arrived[half, step].astype(f32)
        final_out[half, blk, grp] = (total * scale).astype(bf16)
        slot = final_out.at[half, blk, grp]

        def send(step, carry):
            copy(
                slot, slot, a_send.at[half, step], a_recv.at[half, step],
                lax.rem(grp + step, n_grp), blk,
            ).start()
            return carry
        lax.fori_loop(1, n_grp, send, 0)
        spread(half, grp)

    share(0)

    def small_start(step, carry):
        to = lax.rem(blk + step, n_blk)
        copy(small.at[to], small_in.at[step], s_send.at[step], s_recv.at[step], grp, to).start()
        return carry
    lax.fori_loop(1, n_blk, small_start, 0)
    to_before.wait_recv()
    to_after.wait_recv()
    right = right_ref[1].astype(f32)
    right = right + jnp.where(blk > 0, edge[0].astype(f32), 0.0)
    right = right + jnp.where(blk < n_blk - 1, edge[1].astype(f32), 0.0)
    panels[1, blk] = right.astype(bf16)
    mine_g[...] = right.astype(bf16)
    share(1)
    forward(0)
    multiply(0)
    forward(1)
    multiply(1)
    combine(0)
    small_sum = small[blk].astype(f32)
    for step in range(1, n_blk):
        slot = small_in.at[step]
        copy(slot, slot, s_send.at[step], s_recv.at[step], grp, blk).wait_recv()
        small_sum = small_sum + small_in[step].astype(f32)
    small_z[grp] = small_sum.astype(bf16)

    def small_across(step, carry):
        slot = small_z.at[grp]
        copy(slot, slot, sz_send.at[step], sz_recv.at[step], lax.rem(grp + step, n_grp), blk).start()
        return carry
    lax.fori_loop(1, n_grp, small_across, 0)

    combine(1)
    for half in range(2):
        def pass_on(step, carry):
            part = lax.rem(grp + n_grp - step, n_grp)
            slot = final_out.at[half, blk, part]
            copy(slot, slot, a_send.at[half, step], a_recv.at[half, step], grp, blk).wait_recv()
            spread(half, part)
            return carry
        lax.fori_loop(1, n_grp, pass_on, 0)

    def small_take(step, carry):
        slot = small_z.at[lax.rem(grp + n_grp - step, n_grp)]
        copy(slot, slot, sz_send.at[step], sz_recv.at[step], grp, blk).wait_recv()
        return carry
    lax.fori_loop(1, n_grp, small_take, 0)
    small_total = small_z[0].astype(f32)
    for group in range(1, n_grp):
        small_total = small_total + small_z[group].astype(f32)
    small_out[blk] = small_total.astype(bf16)

    def small_spread(step, carry):
        slot = small_out.at[blk]
        copy(
            slot, slot, sa_send.at[step], sa_recv.at[step], grp, lax.rem(blk + step, n_blk)
        ).start()
        return carry
    lax.fori_loop(1, n_blk, small_spread, 0)
    def hand_on(index, carry):
        half, rest = index // n_grp, lax.rem(index, n_grp)
        part = lax.rem(grp + n_grp - rest, n_grp)

        def hand(step, inner):
            slot = final_out.at[half, origin(step), part]
            copy(
                slot, slot, p_send.at[half, part, step], p_recv.at[half, part, step], grp, plane(step)
            ).wait_recv()
            copy(
                slot, slot, q_send.at[half, part, step], q_recv.at[half, part, step], grp, twin
            ).start()
            return inner
        return lax.fori_loop(1, chips, hand, carry)
    emb_out[...] = lax.dot_general(
        left_ref[...], w_left_ref[...], (((1,), (1,)), ((), ())), preferred_element_type=f32
    )
    emb_out[...] += lax.dot_general(
        mine_g[...], w_right_ref[...], (((1,), (1,)), ((), ())), preferred_element_type=f32
    )
    lax.fori_loop(0, 2 * n_grp, hand_on, 0)

    def finish(index, carry):
        half, part = index // n_grp, lax.rem(index, n_grp)

        def end(step, inner):
            slot = final_out.at[half, lax.rem(chip + chips - step, chips) * 2 + 1 - core, part]
            copy(
                slot, slot, q_send.at[half, part, step], q_recv.at[half, part, step], grp, twin
            ).wait()
            return inner
        lax.fori_loop(0, chips, end, 0)

        def sent(step, inner):
            slot = final_out.at[half, blk, part]
            copy(
                slot, slot, p_send.at[half, part, step], p_recv.at[half, part, step], grp, plane(step)
            ).wait_send()
            return inner
        return lax.fori_loop(1, chips, sent, carry)
    lax.fori_loop(0, 2 * n_grp, finish, 0)

    to_before.wait_send()
    to_after.wait_send()

    def small_end(step, carry):
        slot = small_out.at[lax.rem(blk + n_blk - step, n_blk)]
        copy(slot, slot, sa_send.at[step], sa_recv.at[step], grp, blk).wait()
        copy(small.at[0], small_in.at[0], s_send.at[step], s_recv.at[step], grp, blk).wait_send()
        return carry
    lax.fori_loop(1, n_blk, small_end, 0)

    def small_end_z(step, carry):
        slot = small_z.at[0]
        copy(slot, slot, sz_send.at[step], sz_recv.at[step], grp, blk).wait_send()
        return carry
    lax.fori_loop(1, n_grp, small_end_z, 0)
    for half in range(2):
        def g_done(step, carry):
            slot = panels.at[half, blk]
            copy(slot, slot, g_send.at[half, step], g_recv.at[half, step], grp, plane(step)).wait_send()
            return carry
        lax.fori_loop(1, chips, g_done, 0)

        def gf_done(step, carry):
            slot = panels.at[half, blk]
            copy(slot, slot, gf_send.at[half, step], gf_recv.at[half, step], grp, twin).wait_send()
            return carry
        lax.fori_loop(0, chips, gf_done, 0)

        def z_done(step, carry):
            slot = partial.at[half, 0]
            copy(slot, slot, z_send.at[half, step], z_recv.at[half, step], grp, blk).wait_send()
            slot = final_out.at[half, blk, 0]
            copy(slot, slot, a_send.at[half, step], a_recv.at[half, step], grp, blk).wait_send()
            return carry
        lax.fori_loop(1, n_grp, z_done, 0)


def reduce_grads(n_grp, n_blk, scale, left_grad, right_part, emb_cols, w_left, w_right, sums):
    panel, hidden = left_grad.shape
    depth = emb_cols.shape[2]
    wide = w_left.shape[0]
    chips = n_blk // 2
    width = hidden // n_grp
    share_of = -(-(sums.shape[0] // 16 * (hidden // 128)) // n_blk)
    bf16 = jnp.bfloat16
    dma = pltpu.SemaphoreType.DMA
    return pl.pallas_call(
        functools.partial(reduce_kernel, n_grp, n_blk, scale),
        out_shape=(
            jax.ShapeDtypeStruct((panel, wide), jnp.float32),
            jax.ShapeDtypeStruct((2, n_blk, n_grp, depth, width), bf16),
            jax.ShapeDtypeStruct((n_blk, share_of, 16, 128), bf16),
        ),
        in_specs=[pl.BlockSpec(memory_space=pltpu.VMEM)] * 6,
        out_specs=[pl.BlockSpec(memory_space=pltpu.VMEM)] * 3,
        scratch_shapes=[
            pltpu.VMEM((2, panel, hidden), bf16),
            pltpu.VMEM((2, n_blk, panel, hidden), bf16),
            pltpu.VMEM((2, n_grp, depth, width), bf16),
            pltpu.VMEM((2, n_grp, depth, width), bf16),
            pltpu.VMEM((panel, hidden), bf16),
            pltpu.VMEM((n_blk, share_of, 16, 128), bf16),
            pltpu.VMEM((n_blk, share_of, 16, 128), bf16),
            pltpu.VMEM((n_grp, share_of, 16, 128), bf16),
            dma((2,)), dma((2,)),
            dma((2, chips)), dma((2, chips)), dma((2, chips)), dma((2, chips)),
            dma((2, n_grp)), dma((2, n_grp)), dma((2, n_grp)), dma((2, n_grp)),
            dma((2, n_grp, chips)), dma((2, n_grp, chips)),
            dma((2, n_grp, chips)), dma((2, n_grp, chips)),
            dma((n_blk,)), dma((n_blk,)), dma((n_grp,)), dma((n_grp,)), dma((n_blk,)), dma((n_blk,)),
        ],
        compiler_params=pltpu.CompilerParams(
            collective_id=1, has_side_effects=True, vmem_limit_bytes=40 * 1024 * 1024
        ),
        name="reduce_grads",
    )(left_grad, right_part, emb_cols, w_left, w_right, sums)


def unpack_kernel(scale, pieces_ref, small_ref, left_out, right_out, bias_out, middle_out, final_out):
    f32 = jnp.float32
    blocks, n_grp, depth, width = pieces_ref.shape[1:]
    for half, out in enumerate((left_out, right_out)):
        for block in range(blocks):
            for part in range(n_grp):
                out[block * depth:(block + 1) * depth, part * width:(part + 1) * width] = (
                    pieces_ref[half, block, part].astype(f32)
                )

    @pl.when(pl.program_id(0) == 0)
    def _():
        share_of = small_ref.shape[1]
        upper = middle_out.shape[1]
        deep = upper // 16 + 1

        def tile(down, across):
            at = across * deep + down
            return small_ref[at // share_of, at % share_of].astype(f32) * scale

        for across in range(middle_out.shape[0] // 128):
            lanes = slice(across * 128, (across + 1) * 128)
            rows = jnp.concatenate([tile(down, across) for down in range(deep - 1)], axis=0)
            middle_out[lanes, :] = rows.T
            bias_out[:, lanes] = tile(deep - 1, across)[0:1, :]
        final_out[...] = tile(deep - 1, 0)[1:2, 0:upper]


def unpack_grads(scale, pieces, small, hidden, upper):
    _, n_blk, n_grp, depth, width = pieces.shape
    steps = math.gcd(n_blk, 4)
    blocks = n_blk // steps
    f32 = jnp.float32
    rows = blocks * depth
    return pl.pallas_call(
        functools.partial(unpack_kernel, scale),
        grid=(steps,),
        out_shape=(
            jax.ShapeDtypeStruct((n_blk * depth, hidden), f32),
            jax.ShapeDtypeStruct((n_blk * depth, hidden), f32),
            jax.ShapeDtypeStruct((1, hidden), f32),
            jax.ShapeDtypeStruct((hidden, upper), f32),
            jax.ShapeDtypeStruct((1, upper), f32),
        ),
        in_specs=[
            pl.BlockSpec((2, blocks, n_grp, depth, width), lambda i: (0, i, 0, 0, 0)),
            pl.BlockSpec(small.shape, lambda i: (0, 0, 0, 0)),
        ],
        out_specs=[
            pl.BlockSpec((rows, hidden), lambda i: (i, 0)),
            pl.BlockSpec((rows, hidden), lambda i: (i, 0)),
            pl.BlockSpec((1, hidden), lambda i: (0, 0)),
            pl.BlockSpec((hidden, upper), lambda i: (0, 0)),
            pl.BlockSpec((1, upper), lambda i: (0, 0)),
        ],
        compiler_params=pltpu.CompilerParams(vmem_limit_bytes=24 * 1024 * 1024),
        name="unpack_grads",
    )(pieces, small)


def gather_kernel(
    n_blk,
    emb_ref, w_left_ref, w_right_ref, ids_ref, target_ref, block_ref, count_ref,
    left_out, right_out, ids_out, target_out, emb_out,
    emb_cols, ids_mine, target_mine, target_in, w_both, w_sem,
    e_send, e_recv, t_send, t_recv, r_send, r_recv, i_send, i_recv,
):
    f32, bf16 = jnp.float32, jnp.bfloat16
    grp, blk = lax.axis_index("grp"), lax.axis_index("blk")
    depth = emb_out.shape[2]
    slots, fold, lanes = target_ref.shape
    before, after = lax.rem(blk + n_blk - 1, n_blk), lax.rem(blk + 1, n_blk)

    def copy(src, dst, send, recv, blk_to):
        return pltpu.make_async_remote_copy(
            src_ref=src, dst_ref=dst, send_sem=send, recv_sem=recv,
            device_id=(grp, blk_to), device_id_type=MESH,
        )

    fetch_right = pltpu.make_async_copy(w_right_ref, w_both.at[1], w_sem.at[1])
    fetch_left = pltpu.make_async_copy(w_left_ref, w_both.at[0], w_sem.at[0])
    fetch_right.start()
    fetch_left.start()
    barrier = pltpu.get_barrier_semaphore()

    def greet(step, carry):
        pl.semaphore_signal(
            barrier, inc=1, device_id=(grp, lax.rem(blk + step, n_blk)), device_id_type=MESH
        )
        return carry
    lax.fori_loop(1, n_blk, greet, 0)

    for to in range(n_blk):
        emb_cols[to] = emb_ref[:, to * depth:(to + 1) * depth]
    ids_mine[...] = jnp.broadcast_to(ids_ref[...], ids_mine.shape)
    ids_out[1] = ids_mine[...]

    pl.semaphore_wait(barrier, n_blk - 1)

    def send_emb(step, carry):
        to = lax.rem(blk + step, n_blk)
        copy(emb_cols.at[to], emb_out.at[blk], e_send.at[step], e_recv.at[step], to).start()
        return carry
    lax.fori_loop(1, n_blk, send_emb, 0)

    def sum_pairs(to):
        for offset in range(3):
            total = jnp.zeros((fold, lanes), f32)
            number = jnp.zeros((8, lanes), f32)
            for slot in range(slots):
                row, col = block_ref[slot, 0], block_ref[slot, 1]
                hit = (row == to) & (col - row == offset - 1) & (slot < count_ref[0, 0])
                weight = jnp.where(hit, 1.0, 0.0).astype(f32)
                total = total + weight * target_ref[slot]
                number = number + weight
            target_mine[to, offset, 0:fold, :] = total
            target_mine[to, offset, fold:fold + 8, :] = number

    def send_targets(step, carry):
        to = lax.rem(blk + step, n_blk)
        sum_pairs(to)
        copy(target_mine.at[to], target_in.at[step], t_send.at[step], t_recv.at[step], to).start()
        return carry
    lax.fori_loop(1, n_blk, send_targets, 0)
    fetch_right.wait()
    right_out[1] = jnp.dot(
        emb_ref[...], w_both[1], preferred_element_type=f32
    ).astype(bf16)
    exchanges = [
        copy(right_out.at[1], right_out.at[2], r_send.at[0], r_recv.at[0], before),
        copy(right_out.at[1], right_out.at[0], r_send.at[1], r_recv.at[1], after),
        copy(ids_mine, ids_out.at[2], i_send.at[0], i_recv.at[0], before),
        copy(ids_mine, ids_out.at[0], i_send.at[1], i_recv.at[1], after),
    ]
    for exchange in exchanges:
        exchange.start()

    fetch_left.wait()
    left_out[...] = jnp.dot(emb_ref[...], w_both[0], preferred_element_type=f32).astype(bf16)
    emb_out[blk] = emb_cols[blk]
    sum_pairs(blk)
    target_out[...] = target_mine[blk]

    def take_targets(step, carry):
        slot = target_in.at[step]
        copy(slot, slot, t_send.at[step], t_recv.at[step], blk).wait_recv()
        target_out[...] += target_in[step]
        return carry
    lax.fori_loop(1, n_blk, take_targets, 0)

    def finish(step, carry):
        slot = emb_out.at[lax.rem(blk + n_blk - step, n_blk)]
        copy(slot, slot, e_send.at[step], e_recv.at[step], blk).wait()
        copy(target_mine.at[0], target_in.at[0], t_send.at[step], t_recv.at[step], blk).wait_send()
        return carry
    lax.fori_loop(1, n_blk, finish, 0)
    for exchange in exchanges:
        exchange.wait()


def gather_panels(n_blk, emb, w_left, w_right, ids, targets, blocks, counts):
    f32, bf16 = jnp.float32, jnp.bfloat16
    panel, wide = emb.shape
    hidden = w_left.shape[1]
    fold, lanes = targets.shape[1:]
    depth = wide // n_blk
    dma = pltpu.SemaphoreType.DMA
    hbm = pl.BlockSpec(memory_space=pl.ANY)
    vmem, smem = pl.BlockSpec(memory_space=pltpu.VMEM), pl.BlockSpec(memory_space=pltpu.SMEM)
    return pl.pallas_call(
        functools.partial(gather_kernel, n_blk),
        out_shape=(
            jax.ShapeDtypeStruct((panel, hidden), bf16),
            jax.ShapeDtypeStruct((3, panel, hidden), bf16),
            jax.ShapeDtypeStruct((3, panel, 128), f32),
            jax.ShapeDtypeStruct((3, fold + 8, lanes), f32),
            jax.ShapeDtypeStruct((n_blk, panel, depth), bf16),
        ),
        in_specs=[vmem, hbm, hbm, vmem, vmem, smem, smem],
        out_specs=[vmem] * 5,
        scratch_shapes=[
            pltpu.VMEM((n_blk, panel, depth), bf16),
            pltpu.VMEM((panel, 128), f32),
            pltpu.VMEM((n_blk, 3, fold + 8, lanes), f32),
            pltpu.VMEM((n_blk, 3, fold + 8, lanes), f32),
            pltpu.VMEM((2, wide, hidden), bf16),
            dma((2,)),
            dma((n_blk,)), dma((n_blk,)), dma((n_blk,)), dma((n_blk,)),
            dma((2,)), dma((2,)), dma((2,)), dma((2,)),
        ],
        compiler_params=pltpu.CompilerParams(
            collective_id=2, has_side_effects=True, vmem_limit_bytes=32 * 1024 * 1024
        ),
        name="gather_panels",
    )(emb, w_left, w_right, ids, targets, blocks, counts)


def local(
    embeddings, cluster_ids, block_list, block_counts, pair_targets,
    w_left, w_right, hidden_bias, w_middle, w_final,
):
    f32, bf16 = jnp.float32, jnp.bfloat16
    n_blk = lax.axis_size("blk")
    n_grp = lax.axis_size("grp")
    emb = embeddings[0]
    panel = emb.shape[0]
    slots = block_list.shape[1]
    hidden = w_left.shape[1]
    upper = w_middle.shape[1]
    fold = panel * panel // 128
    targets = pair_targets[0].reshape(slots, panel, panel // fold, fold)
    targets = targets.transpose(0, 3, 2, 1).reshape(slots, fold, 128)
    ids = cluster_ids[0].astype(f32)
    left, right, col_ids, targets, emb_cols = gather_panels(
        n_blk, emb, w_left, w_right, ids[:, None], targets, block_list[0], block_counts
    )
    left_grad, right_part, sums = pair_grads(
        left, right, hidden_bias, ids[None, :], col_ids, targets, w_middle, w_final
    )
    scale = 1.0 / math.sqrt(n_grp * n_blk * slots * panel)
    grad_local, pieces, small = reduce_grads(
        n_grp, n_blk, scale, left_grad, right_part, emb_cols, w_left, w_right, sums
    )
    grad_left, grad_right, grad_bias, grad_middle, grad_final = unpack_grads(
        scale, pieces, small, hidden, upper
    )
    return grad_local[None], grad_left, grad_right, grad_bias[0], grad_middle, grad_final[0]


def solution(mesh):
    return jax.shard_map(
        local,
        mesh=mesh,
        in_specs=(
            P("grp", "blk", None), P("grp", "blk"), P("grp", "blk", None), P("grp", "blk"),
            P("grp", "blk", None), P(), P(), P(), P(), P(),
        ),
        out_specs=(P("grp", "blk", None), P(), P(), P(), P(), P()),
        check_vma=False,
    )
```
